256 devices in a mesh: comp: 4 (over z_hi), dom: 32 (over y, x, core), lev: 2 (over z_lo).
Axes of the slice: x: 4, y: 4, z: 8 (z_hi: 4, z_lo: 2; z = z_hi * 2 + z_lo), core: 2. Of those that a mesh axis runs over, the one named last changes fastest.
Arguments:
- air_profile_vector: float32 [144, 262144], P(None, ('comp', 'dom', 'lev')), may hold values from -6 to 6
- profile_pass_kind: int32 [262144], P(('comp', 'dom', 'lev')), may hold values from 1 to 3, as said below
- position_profile_map: int32 [262144], P(('comp', 'dom', 'lev')), may hold values from 0 to 1023, as said below
- sunlight_aerosol_drive: float32 [144, 262144], P(None, ('comp', 'dom', 'lev')), may hold values from -6 to 6
- profile_link_operator: float32 [144, 144], replicated, may hold values from -0.5 to 0.5
- bottom_warmth_seen: float32 [262144], P(('comp', 'dom', 'lev')), may hold values from -6 to 6
- intersect_sender_index: int32 [8192, 256], P(('comp', 'dom', 'lev')), may hold values from 0 to 1023
- intersect_share: float32 [8192, 256], P(('comp', 'dom', 'lev')), may hold values from 0.1 to 1
- intersect_receiver_tile: int32 [8192, 256], P(('comp', 'dom', 'lev')), may hold values from 0 to 8191
- marine_warmth_departure: float32 [80, 1024, 1024], P('lev', ('comp', 'dom')), may hold values from -6 to 6
- earlier_bottom_inflow: float32 [1024, 1024], P(('comp', 'dom')), may hold values from -6 to 6
- marine_tile_indicator: int32 [1024, 1024], P(('comp', 'dom')), may hold values 0 or 1
Outputs:
- air_profile_updated: float32 [144, 262144], P(None, ('comp', 'dom', 'lev'))
- ocean_temp_out: float32 [80, 1024, 1024], P('lev', ('comp', 'dom'))
- marine_warming_rate: float32 [1024, 1024], P(('comp', 'dom'))
- air_bottom_warmth: float32 [262144], P(('comp', 'dom', 'lev'))
The draws below stay inside these ranges and needn't reach their ends.
Inputs may be any that keep to these rules, and one draw needn't show every extreme that they name: `profile_pass_kind`: each column's number of physics sweeps; some device holds columns of class 3. `position_profile_map`: on each device the first 512 entries are distinct local columns of the device itself; the last 512 are distinct local columns of the device half the dom axis away (same comp and lev), namely those that device does not keep; so every dynamics column is held by exactly one slot.
All inputs are finite; a program needn't handle non-finite values. No bound on the sum of `marine_tile_indicator` on one device may be relied on, other than what follows from the above.
Results may differ from the reference program's by a relative error of at most 0.0001.
Values sent between devices are 32-bit elements; how exact they have to be, the bound alone decides.
No kernel may reach another device: no remote copies, remote signals or barrier semaphores. Data moves between devices by JAX's collectives and lax.ppermute only.
A program may use at most 64 MiB of HBM per device.

```python
import jax
import jax.numpy as jnp
from jax import lax

ATMOS_LEVELS = 72
SEA_DEPTH_TIERS = 80
CLASSES = 3
STEPS = 4
COLS_DEV = 1024
SEA_SPAN_ALONG = 1024
SLOTS = 256
ATMOS_COLUMNS = 262144
SEA_LINES_TOTAL = 1024
OCELL = 8192
N_COMP = 4
N_DOM = 32
N_LEV = 2


def draw_profile_pass_kind(key, part):
    key = jax.random.fold_in(key, 5)
    device_count = ATMOS_COLUMNS // COLS_DEV
    first_key, second_key = jax.random.split(key)
    level = jax.random.randint(first_key, (device_count, 1), 1, CLASSES + 1)
    level = level.at[0, 0].set(CLASSES)
    column_level = jax.random.randint(second_key, (device_count, COLS_DEV), 1, CLASSES + 1)
    return jnp.maximum(level, column_level).reshape(ATMOS_COLUMNS).astype(jnp.int32)


def draw_position_profile_map(key, part):
    key = jax.random.fold_in(key, 9)
    device_count = ATMOS_COLUMNS // COLS_DEV
    device_keys = jax.random.split(key, device_count)
    orders = jax.vmap(lambda single: jax.random.permutation(single, COLS_DEV))(device_keys).astype(jnp.int32)
    grid = orders.reshape(N_COMP, N_DOM, N_LEV, COLS_DEV)
    rolled = jnp.roll(grid, N_DOM // 2, axis=1)
    half_cols = COLS_DEV // 2
    joined = jnp.concatenate([grid[..., :half_cols], rolled[..., half_cols:]], axis=-1)
    return joined.reshape(ATMOS_COLUMNS).astype(jnp.int32)


def with_ends(array, key, low, largest):
    spot = [jax.random.randint(jax.random.fold_in(key, axis), (), 0, length) for axis, length in enumerate(array.shape)]
    longest = array.shape.index(max(array.shape))
    neighbour = spot[:longest] + [(spot[longest] + 1) % array.shape[longest]] + spot[longest + 1:]
    return array.at[tuple(spot)].set(low).at[tuple(neighbour)].set(largest)


def steps_of(rng, extent, cuts, low, largest):
    loudness, own = 1.0, jax.random.fold_in(rng, 6)
    for axis_at, parts in cuts:
        draws = jnp.exp(jax.random.uniform(jax.random.fold_in(own, axis_at), (parts,), jnp.float32, low / len(cuts), largest / len(cuts)))
        loudness = loudness * jnp.repeat(draws, extent[axis_at] // parts).reshape([-1 if axis == axis_at else 1 for axis in range(len(extent))])
    return loudness


def normal_values(stream_key, shape, deviation, most, cuts=(), kind=jnp.bfloat16):
    array = jax.random.normal(stream_key, shape, jnp.float32) * deviation
    if len(cuts) > 0:
        array = steps_of(stream_key, shape, cuts, -0.22, 0.18) * array
    return jnp.clip(array, min=-most, max=most).astype(kind)


def setup_inputs(seed: int = 0) -> dict:
    key_list = jax.random.split(jax.random.key(seed), 13)
    return {
        "air_profile_vector": normal_values(key_list[0], (2 * ATMOS_LEVELS, ATMOS_COLUMNS), 1.0, 6.0, ((1, 256),), jnp.float32),
        "profile_pass_kind": draw_profile_pass_kind(jax.random.fold_in(key_list[12], 71), 0),
        "position_profile_map": draw_position_profile_map(jax.random.fold_in(key_list[12], 71), 0),
        "sunlight_aerosol_drive": normal_values(key_list[3], (2 * ATMOS_LEVELS, ATMOS_COLUMNS), 0.7, 6.0, ((1, 256),), jnp.float32),
        "profile_link_operator": normal_values(key_list[4], (2 * ATMOS_LEVELS, 2 * ATMOS_LEVELS), (2 * ATMOS_LEVELS) ** -0.5, 0.5, (), jnp.float32),
        "bottom_warmth_seen": normal_values(key_list[5], (ATMOS_COLUMNS,), 1.0, 6.0, ((0, 256),), jnp.float32),
        "intersect_sender_index": with_ends(jax.random.randint(key_list[6], (N_COMP * N_DOM * N_LEV * N_DOM, SLOTS), 0, COLS_DEV), jax.random.fold_in(key_list[6], 1), 0, COLS_DEV - 1).astype(jnp.int32),
        "intersect_share": jnp.clip(0.1 + 0.9 * jax.random.uniform(key_list[7], (N_COMP * N_DOM * N_LEV * N_DOM, SLOTS), jnp.float32) ** steps_of(key_list[7], (N_COMP * N_DOM * N_LEV * N_DOM, SLOTS), ((0, 256),), -0.2, 0.2), 0.1, 1.0),
        "intersect_receiver_tile": with_ends(jax.random.randint(key_list[8], (N_COMP * N_DOM * N_LEV * N_DOM, SLOTS), 0, OCELL), jax.random.fold_in(key_list[8], 1), 0, OCELL - 1).astype(jnp.int32),
        "marine_warmth_departure": normal_values(key_list[9], (SEA_DEPTH_TIERS, SEA_LINES_TOTAL, SEA_SPAN_ALONG), 1.0, 6.0, ((0, 2), (1, 128)), jnp.float32),
        "earlier_bottom_inflow": normal_values(key_list[10], (SEA_LINES_TOTAL, SEA_SPAN_ALONG), 1.0, 6.0, ((0, 128),), jnp.float32),
        "marine_tile_indicator": with_ends((jax.random.randint(key_list[11], (SEA_LINES_TOTAL, SEA_SPAN_ALONG), 0, 4) < 3).astype(jnp.int32), jax.random.fold_in(key_list[11], 1), 0, 1),
    }


surface_exchange_factor = 0.8
humidity_exchange_factor = 0.5
tendency_scale = 0.5
horizontal_rate = 0.15
vertical_rate = 0.1
flux_gain = 0.5


def column_physics(state, forcing, classes, profile_link_operator):
    for sweep_index in range(CLASSES):
        drive = jnp.dot(profile_link_operator, state, precision=lax.Precision.HIGHEST, preferred_element_type=jnp.float32) + forcing
        state = state + jnp.where(classes[None, :] > sweep_index, tendency_scale * jnp.tanh(drive), jnp.float32(0.0))
    return state


def marine_advance(theta_profile, earlier_bottom_inflow, marine):
    bordered = jnp.pad(theta_profile, ((1, 1), (1, 1), (0, 0)))
    sideways = bordered[1:-1, 2:] + bordered[1:-1, :-2] + jnp.roll(theta_profile, 1, 2) + jnp.roll(theta_profile, -1, 2) - 4.0 * theta_profile
    upright = bordered[2:, 1:-1] + bordered[:-2, 1:-1] - 2.0 * theta_profile
    increment = horizontal_rate * sideways + vertical_rate * upright
    increment = increment.at[0].add(flux_gain * earlier_bottom_inflow)
    return theta_profile + marine * increment


def reference(air_profile_vector, profile_pass_kind, position_profile_map, sunlight_aerosol_drive, profile_link_operator, bottom_warmth_seen, intersect_sender_index, intersect_share, intersect_receiver_tile, marine_warmth_departure, earlier_bottom_inflow, marine_tile_indicator):
    comp_index = jnp.arange(N_COMP, dtype=jnp.int32)[:, None, None, None]
    dom_index = jnp.arange(N_DOM, dtype=jnp.int32)[None, :, None, None]
    lev_index = jnp.arange(N_LEV, dtype=jnp.int32)[None, None, :, None]
    slot_index = jnp.arange(COLS_DEV, dtype=jnp.int32)[None, None, None, :]
    from_dom = jnp.where(slot_index < COLS_DEV // 2, dom_index, (dom_index - N_DOM // 2) % N_DOM)
    span_grid = position_profile_map.reshape(N_COMP, N_DOM, N_LEV, COLS_DEV)
    sources = (((comp_index * N_DOM + from_dom) * N_LEV + lev_index) * COLS_DEV + span_grid).reshape(-1).astype(jnp.int32)
    regrouped = column_physics(jnp.take(air_profile_vector, sources, axis=1), sunlight_aerosol_drive, jnp.take(profile_pass_kind, sources), profile_link_operator)
    air_profile_updated = jnp.zeros_like(air_profile_vector).at[:, sources].set(regrouped)
    heat_flux = surface_exchange_factor * (air_profile_updated[ATMOS_LEVELS - 1] - bottom_warmth_seen) + humidity_exchange_factor * air_profile_updated[2 * ATMOS_LEVELS - 1]
    base = ((comp_index * N_DOM + dom_index) * N_LEV + lev_index) * COLS_DEV
    source_grid = intersect_sender_index.reshape(N_COMP, N_DOM, N_LEV, N_DOM, SLOTS)
    weight_matrix_grid = intersect_share.reshape(N_COMP, N_DOM, N_LEV, N_DOM, SLOTS)
    source_column_global = (base[..., None] + source_grid).astype(jnp.int32)
    target_grid = intersect_receiver_tile.reshape(N_COMP, N_DOM, N_LEV, N_DOM, SLOTS).transpose(0, 3, 2, 1, 4)
    target_block = comp_index[..., None] * N_DOM + jnp.arange(N_DOM, dtype=jnp.int32)[None, None, None, :, None]
    target_global = (target_block * OCELL + target_grid).astype(jnp.int32)
    pieces = weight_matrix_grid * jnp.take(heat_flux, source_column_global)
    marine_warming_rate = jax.ops.segment_sum(pieces.reshape(-1), target_global.reshape(-1), num_segments=N_COMP * N_DOM * OCELL).reshape(SEA_LINES_TOTAL, SEA_SPAN_ALONG)
    marine = marine_tile_indicator.astype(jnp.float32)[None]
    theta_profile = marine_warmth_departure
    for step_index in range(STEPS):
        theta_profile = marine_advance(theta_profile, earlier_bottom_inflow, marine)
    bottom_boundary = theta_profile[0].reshape(-1)
    gathered_back = jnp.take(bottom_boundary, target_global)
    air_bottom_warmth = jax.ops.segment_sum((weight_matrix_grid * gathered_back).reshape(-1), source_column_global.reshape(-1), num_segments=ATMOS_COLUMNS)
    return (air_profile_updated, theta_profile, marine_warming_rate, air_bottom_warmth)
```

```python
import jax
import jax.numpy as jnp
from jax import lax
from jax.experimental import pallas as pl
from jax.experimental.pallas import tpu as pltpu
from jax.sharding import PartitionSpec as P

STEPS = 4
CLASSES = 3
LANES = 128
SUBLANES = 8

surface_exchange_factor = 0.8
humidity_exchange_factor = 0.5
tendency_scale = 0.5
horizontal_rate = 0.15
vertical_rate = 0.1
flux_gain = 0.5

f32 = jnp.float32
bf16 = jnp.bfloat16
i32 = jnp.int32


def whole():
    return pl.BlockSpec(memory_space=pltpu.VMEM)


def call(body, out_shapes, specs, args, name, microseconds, scratch=(), mib=32, grid=()):
    one = not isinstance(out_shapes, (list, tuple))
    shapes = [out_shapes] if one else list(out_shapes)
    out = pl.pallas_call(
        body,
        out_shape=shapes,
        grid=grid,
        in_specs=specs,
        out_specs=[whole() for _ in shapes],
        scratch_shapes=list(scratch),
        compiler_params=pltpu.CompilerParams(vmem_limit_bytes=mib * 1024 * 1024),
        cost_estimate=pl.CostEstimate(
            flops=0, bytes_accessed=int(microseconds * 3.0e6), transcendentals=0
        ),
        name=name,
    )(*args)
    return out[0] if one else out


def split(value):
    high = value.astype(bf16)
    low = (value - high.astype(f32)).astype(bf16)
    return high, low


def dot_nt(a, b):
    return lax.dot_general(a, b, (((1,), (1,)), ((), ())), preferred_element_type=f32)


def dot_nn(a, b):
    return lax.dot_general(a, b, (((1,), (0,)), ((), ())), preferred_element_type=f32)


def pack_forcing(drive_ref, place_ref, out_ref):
    rows, half = drive_ref.shape
    out_ref[0:rows, :] = drive_ref[...]
    far = place_ref[:, half : 2 * half].astype(f32)
    out_ref[rows : rows + SUBLANES, :] = jnp.broadcast_to(far, (SUBLANES, half))


def pack_ocean(theta_ref, inflow_ref, wet_ref, up_ref, down_ref, level_ref, up_corner_ref, down_corner_ref):
    tiers = theta_ref.shape[0]
    up_ref[0] = inflow_ref[4:8, :]
    down_ref[0] = inflow_ref[0:4, :]
    up_ref[1] = wet_ref[4:8, :].astype(f32)
    down_ref[1] = wet_ref[0:4, :].astype(f32)

    def copy_level(tier, carry):
        up_ref[tier + 2] = theta_ref[tier, 4:8, :]
        down_ref[tier + 2] = theta_ref[tier, 0:4, :]
        return carry

    lax.fori_loop(0, tiers, copy_level, 0, unroll=4)
    base = jnp.where(lax.axis_index("lev") == 0, tiers - STEPS, 0)
    for j in range(STEPS):
        level_ref[j] = theta_ref[base + j]
        up_corner_ref[j] = theta_ref[base + j, 4:8, :]
        down_corner_ref[j] = theta_ref[base + j, 0:4, :]


def across(own, halo):
    span = own.shape[1]
    row = lax.broadcasted_iota(i32, own.shape, 0)
    first, last = row == 0, row == SUBLANES - 1
    own_less, halo_less = pltpu.roll(own, 1, 0), pltpu.roll(halo, 1, 0)
    own_more, halo_more = pltpu.roll(own, SUBLANES - 1, 0), pltpu.roll(halo, SUBLANES - 1, 0)
    own_sum = jnp.where(first, halo_less, own_less) + jnp.where(last, halo_more, own_more)
    own_sum = own_sum + (pltpu.roll(own, 1, 1) + pltpu.roll(own, span - 1, 1))
    halo_sum = jnp.where(first, own_less, halo_less) + jnp.where(last, own_more, halo_more)
    halo_sum = halo_sum + (pltpu.roll(halo, 1, 1) + pltpu.roll(halo, span - 1, 1))
    return own_sum, halo_sum


def top_level(theta_ref, before_ref, after_ref, inflow_ref, wet_ref, out_ref):
    count = STEPS + 1

    def joined(k):
        return jnp.concatenate([after_ref[k], before_ref[k]], axis=0)

    wet = (wet_ref[...].astype(f32), joined(1))
    source = tuple(flux_gain * w * s for w, s in zip(wet, (inflow_ref[...], joined(0))))
    keep = tuple(1.0 - (4 * horizontal_rate + 2 * vertical_rate) * w for w in wet)
    side = tuple(horizontal_rate * w for w in wet)
    rise = tuple(vertical_rate * w for w in wet)
    levels = [(theta_ref[k], joined(k + 2)) for k in range(count)]
    for step in range(1, STEPS + 1):
        fresh = []
        for k in range(count - step):
            sums = across(*levels[k])
            value = []
            for part in range(2):
                vertical = levels[k + 1][part]
                if k > 0:
                    vertical = vertical + levels[k - 1][part]
                new = keep[part] * levels[k][part] + side[part] * sums[part] + rise[part] * vertical
                if k == 0:
                    new = new + source[part]
                value.append(new)
            fresh.append(tuple(value))
        levels = fresh
    out_ref[...] = levels[0][0]


def ocean(
    theta_ref,
    before_ref,
    after_ref,
    level_ref,
    before_corner_ref,
    after_corner_ref,
    inflow_ref,
    wet_ref,
    out_ref,
    even,
    odd,
    keep,
    side,
    rise,
    source,
):
    tiers = theta_ref.shape[0]
    places = tiers + STEPS
    lev = lax.axis_index("lev")
    lower = lev.astype(f32)
    upper = 1.0 - lower

    wet_own = wet_ref[...].astype(f32)
    wet_halo = jnp.concatenate([after_ref[1], before_ref[1]], axis=0)
    flow_halo = jnp.concatenate([after_ref[0], before_ref[0]], axis=0)
    for at, wet, flow in ((0, wet_own, inflow_ref[...]), (8, wet_halo, flow_halo)):
        rows = slice(at, at + 8)
        keep[rows, :] = 1.0 - (4 * horizontal_rate + 2 * vertical_rate) * wet
        side[rows, :] = horizontal_rate * wet
        rise[rows, :] = vertical_rate * wet
        source[rows, :] = (flux_gain * upper) * (wet * flow)

    def gather_level(tier, carry):
        even[tier, 0:8, :] = theta_ref[tier]
        even[tier, 8:12, :] = after_ref[tier + 2]
        even[tier, 12:16, :] = before_ref[tier + 2]
        return carry

    lax.fori_loop(0, tiers, gather_level, 0, unroll=2)
    for j in range(STEPS):
        even[tiers + j, 0:8, :] = level_ref[j]
        even[tiers + j, 8:12, :] = after_corner_ref[j]
        even[tiers + j, 12:16, :] = before_corner_ref[j]

    for step in range(1, STEPS + 1):
        held, fresh = (even, odd) if step % 2 else (odd, even)
        final = step == STEPS

        def advance(at, less, more, less_scale=None, more_scale=None, add_source=False):
            own, halo = held[at, 0:8, :], held[at, 8:16, :]
            sums = across(own, halo)
            for part, start in ((0, 0), (1, 8)):
                if final and part == 1:
                    continue
                rows = slice(start, start + 8)
                a, b = held[less, rows, :], held[more, rows, :]
                if less_scale is not None:
                    a = a * less_scale
                if more_scale is not None:
                    b = b * more_scale
                new = (
                    keep[rows, :] * (own, halo)[part]
                    + side[rows, :] * sums[part]
                    + rise[rows, :] * (a + b)
                )
                if add_source:
                    new = new + source[rows, :]
                if final:
                    out_ref[at] = new
                else:
                    fresh[at, rows, :] = new

        advance(0, places - 1, 1, less_scale=lower, add_source=True)

        def inner(at, carry):
            advance(at, at - 1, at + 1)
            return carry

        lax.fori_loop(1, tiers - 1, inner, 0, unroll=2)
        advance(tiers - 1, tiers - 2, tiers, more_scale=upper)
        for j in range(STEPS - step):
            at = tiers + j + lev * step
            more = jnp.where(at == places - 1, 0, at + 1)
            advance(at, at - 1, more)


def columns(
    state_ref,
    classes_ref,
    place_ref,
    drive_ref,
    far_ref,
    link_ref,
    warmth_ref,
    sender_ref,
    share_ref,
    tile_ref,
    top_ref,
    top_far_ref,
    out_ref,
    payload_ref,
):
    rows, count = state_ref.shape
    half = drive_ref.shape[1]
    levels = rows // 2
    width = 256

    own_drive = jnp.concatenate(split(drive_ref[...]), axis=0)
    far_drive = jnp.concatenate(split(far_ref[0:rows, :]), axis=0)
    own_place = place_ref[:, 0:half]
    far_place = far_ref[rows : rows + 1, :].astype(i32)
    link_high, link_low = split(link_ref[...])
    link_both = jnp.concatenate([link_high, link_low], axis=0)

    flux = []
    for start in range(0, count, width):
        cols = slice(start, start + width)
        target = start + lax.broadcasted_iota(i32, (width, half), 0)
        own_pick = jnp.where(target == own_place, 1.0, 0.0).astype(bf16)
        far_pick = jnp.where(target == far_place, 1.0, 0.0).astype(bf16)
        both = dot_nt(own_drive, own_pick) + dot_nt(far_drive, far_pick)
        forcing = both[0:rows] + both[rows : 2 * rows]
        x = state_ref[:, cols]
        kinds = classes_ref[:, cols]
        for k in range(CLASSES):
            high, low = split(x)
            product = dot_nn(link_both, high)
            drive = product[0:rows] + (product[rows : 2 * rows] + dot_nn(link_high, low)) + forcing
            x = x + jnp.where(kinds > k, tendency_scale * jnp.tanh(drive), 0.0)
        out_ref[:, cols] = x
        flux.append(
            surface_exchange_factor * (x[levels - 1 : levels, :] - warmth_ref[:, cols])
            + humidity_exchange_factor * x[rows - 1 : rows, :]
        )
    flux = jnp.concatenate(flux, axis=1)

    entry_rows, slots = sender_ref.shape
    blocks = [
        (slice(r, r + SUBLANES), slice(c, c + LANES))
        for r in range(0, entry_rows, SUBLANES)
        for c in range(0, slots, LANES)
    ]
    block_shape = (SUBLANES, LANES)

    def picked(table, lane):
        spread = jnp.broadcast_to(table, block_shape)
        return jnp.take_along_axis(spread, lane, axis=1, mode="promise_in_bounds")

    lanes = [sender_ref[b] & (LANES - 1) for b in blocks]
    keys = [sender_ref[b] >> 7 for b in blocks]
    found = [jnp.zeros(block_shape, f32) for _ in blocks]
    for r in range(count // LANES):
        table = flux[:, r * LANES : (r + 1) * LANES]
        found = [jnp.where(k == r, picked(table, l), v) for k, l, v in zip(keys, lanes, found)]
    for b, v in zip(blocks, found):
        payload_ref[b] = share_ref[b] * v

    lines, span = top_ref.shape
    surface = jnp.where(lax.axis_index("lev") == 0, top_ref[...], top_far_ref[...])
    chunks = span // LANES
    lanes = [tile_ref[b] & (LANES - 1) for b in blocks]
    keys = [tile_ref[b] >> 7 for b in blocks]
    found = [jnp.zeros(block_shape, f32) for _ in blocks]
    for r in range(lines):
        for c in range(chunks):
            table = surface[r : r + 1, c * LANES : (c + 1) * LANES]
            found = [
                jnp.where(k == r * chunks + c, picked(table, l), v)
                for k, l, v in zip(keys, lanes, found)
            ]
    for (r, c), v in zip(blocks, found):
        payload_ref[r, slots + c.start : slots + c.stop] = v


def entry_sum(index_row, value_row, groups, order):
    entries = index_row.shape[1]
    group = order(index_row)
    hit = lax.broadcasted_iota(i32, (groups, entries), 0) == group
    high = value_row.astype(bf16).astype(f32)
    low = value_row - high
    weighted = jnp.concatenate(
        [jnp.where(hit, high, 0.0).astype(bf16), jnp.where(hit, low, 0.0).astype(bf16)], axis=0
    )
    lane = index_row & (LANES - 1)
    lane_hit = lax.broadcasted_iota(i32, (LANES, entries), 0) == lane
    return dot_nt(weighted, jnp.where(lane_hit, 1.0, 0.0).astype(bf16))


def add_flux(received_ref, tile_ref, out_ref):
    entry_rows, slots = tile_ref.shape
    lines, span = out_ref.shape
    chunks = span // LANES
    groups = lines * chunks
    total = jnp.zeros((2 * groups, LANES), f32)
    for d in range(entry_rows):
        total = total + entry_sum(
            tile_ref[d : d + 1, :],
            received_ref[d : d + 1, 0:slots],
            groups,
            lambda t: ((t >> 7) & (chunks - 1)) * lines + (t >> 10),
        )
    total = total[0:groups] + total[groups:]
    for c in range(chunks):
        out_ref[:, c * LANES : (c + 1) * LANES] = total[c * lines : (c + 1) * lines]


def add_warmth(received_ref, sender_ref, share_ref, out_ref):
    entry_rows, slots = sender_ref.shape
    groups = out_ref.shape[0]
    total = jnp.zeros((2 * groups, LANES), f32)
    for d in range(entry_rows):
        total = total + entry_sum(
            sender_ref[d : d + 1, :],
            received_ref[d : d + 1, slots : 2 * slots] * share_ref[d : d + 1, :],
            groups,
            lambda t: t >> 7,
        )
    out_ref[...] = total[0:groups] + total[groups:]


def on_device(
    air_profile_vector,
    profile_pass_kind,
    position_profile_map,
    sunlight_aerosol_drive,
    profile_link_operator,
    bottom_warmth_seen,
    intersect_sender_index,
    intersect_share,
    intersect_receiver_tile,
    marine_warmth_departure,
    earlier_bottom_inflow,
    marine_tile_indicator,
):
    rows, count = air_profile_vector.shape
    half = count // 2
    tiers, lines, span = marine_warmth_departure.shape
    entry_rows, slots = intersect_sender_index.shape
    n_dom, n_lev = lax.axis_size("dom"), lax.axis_size("lev")
    n_block = lax.axis_size("comp") * n_dom
    place = position_profile_map.reshape(1, count)

    def shape(*dims):
        return jax.ShapeDtypeStruct(dims, f32)

    packed = call(
        pack_forcing,
        shape(rows + SUBLANES, half),
        [pl.BlockSpec((rows, half), lambda i: (0, 1)), whole()],
        (sunlight_aerosol_drive, place),
        "pack_forcing",
        1.5,
        grid=(1,),
    )
    far = lax.ppermute(packed, "dom", [(i, (i + n_dom // 2) % n_dom) for i in range(n_dom)])

    up, down, level, up_corner, down_corner = call(
        pack_ocean,
        [
            shape(tiers + 2, 4, span),
            shape(tiers + 2, 4, span),
            shape(STEPS, lines, span),
            shape(STEPS, 4, span),
            shape(STEPS, 4, span),
        ],
        [whole()] * 3,
        (marine_warmth_departure, earlier_bottom_inflow, marine_tile_indicator),
        "pack_ocean",
        2.0,
    )
    block_axes = ("comp", "dom")
    all_axes = ("comp", "dom", "lev")
    rising = [(i, i + 1) for i in range(n_block - 1)]
    falling = [(j, i) for i, j in rising]
    other = [(0, 1), (1, 0)]

    def corners(pairs):
        return [(a * n_lev + l, b * n_lev + m) for a, b in pairs for l, m in other]

    before = lax.ppermute(up, block_axes, rising)
    after = lax.ppermute(down, block_axes, falling)
    level = lax.ppermute(level, "lev", other)
    before_corner = lax.ppermute(up_corner, all_axes, corners(rising))
    after_corner = lax.ppermute(down_corner, all_axes, corners(falling))

    part = pl.BlockSpec((STEPS + 3, 4, span), lambda i: (0, 0, 0))
    top = call(
        top_level,
        shape(lines, span),
        [pl.BlockSpec((STEPS + 1, lines, span), lambda i: (0, 0, 0)), part, part, whole(), whole()],
        (marine_warmth_departure, before, after, earlier_bottom_inflow, marine_tile_indicator),
        "top_level",
        2.0,
        grid=(1,),
    )
    top_far = lax.ppermute(top, "lev", [(0, 1)])

    air_profile_updated, payload = call(
        columns,
        [shape(rows, count), shape(entry_rows, 2 * slots)],
        [whole()] * 3 + [pl.BlockSpec((rows, half), lambda i: (0, 0))] + [whole()] * 8,
        (
            air_profile_vector,
            profile_pass_kind.reshape(1, count),
            place,
            sunlight_aerosol_drive,
            far,
            profile_link_operator,
            bottom_warmth_seen.reshape(1, count),
            intersect_sender_index,
            intersect_share,
            intersect_receiver_tile,
            top,
            top_far,
        ),
        "columns",
        6.0,
        grid=(1,),
    )
    received = lax.all_to_all(payload, "dom", split_axis=0, concat_axis=0, tiled=True)

    theta = call(
        ocean,
        shape(tiers, lines, span),
        [whole()] * 8,
        (
            marine_warmth_departure,
            before,
            after,
            level,
            before_corner,
            after_corner,
            earlier_bottom_inflow,
            marine_tile_indicator,
        ),
        "ocean",
        6.0,
        scratch=[pltpu.VMEM((tiers + STEPS, 16, span), f32)] * 2 + [pltpu.VMEM((16, span), f32)] * 4,
    )

    partial_flux = call(
        add_flux,
        shape(lines, span),
        [whole()] * 2,
        (received, intersect_receiver_tile),
        "add_flux",
        2.0,
    )
    marine_warming_rate = partial_flux + lax.ppermute(partial_flux, "lev", other)
    air_bottom_warmth = call(
        add_warmth,
        shape(count // LANES, LANES),
        [whole()] * 3,
        (received, intersect_sender_index, intersect_share),
        "add_warmth",
        2.0,
    ).reshape(count)
    return (air_profile_updated, theta, marine_warming_rate, air_bottom_warmth)


def solution(mesh):
    placed = (
        P(None, ("comp", "dom", "lev")),
        P(("comp", "dom", "lev")),
        P(("comp", "dom", "lev")),
        P(None, ("comp", "dom", "lev")),
        P(),
        P(("comp", "dom", "lev")),
        P(("comp", "dom", "lev"), None),
        P(("comp", "dom", "lev"), None),
        P(("comp", "dom", "lev"), None),
        P("lev", ("comp", "dom"), None),
        P(("comp", "dom"), None),
        P(("comp", "dom"), None),
    )
    return jax.shard_map(
        on_device,
        mesh=mesh,
        in_specs=placed,
        out_specs=(
            P(None, ("comp", "dom", "lev")),
            P("lev", ("comp", "dom"), None),
            P(("comp", "dom"), None),
            P(("comp", "dom", "lev")),
        ),
        check_vma=False,
    )
```

```python
import jax
import jax.numpy as jnp
from jax import lax
from jax.experimental import pallas as pl
from jax.experimental.pallas import tpu as pltpu
from jax.sharding import PartitionSpec as P

STEPS = 4
CLASSES = 3
LANES = 128
SUBLANES = 8

surface_exchange_factor = 0.8
humidity_exchange_factor = 0.5
tendency_scale = 0.5
horizontal_rate = 0.15
vertical_rate = 0.1
flux_gain = 0.5

f32 = jnp.float32
bf16 = jnp.bfloat16
i32 = jnp.int32


def whole():
    return pl.BlockSpec(memory_space=pltpu.VMEM)


def call(body, out_shapes, specs, args, name, microseconds, scratch=(), mib=32, grid=()):
    one = not isinstance(out_shapes, (list, tuple))
    shapes = [out_shapes] if one else list(out_shapes)
    out = pl.pallas_call(
        body,
        out_shape=shapes,
        grid=grid,
        in_specs=specs,
        out_specs=[whole() for _ in shapes],
        scratch_shapes=list(scratch),
        compiler_params=pltpu.CompilerParams(vmem_limit_bytes=mib * 1024 * 1024),
        cost_estimate=pl.CostEstimate(
            flops=0, bytes_accessed=int(microseconds * 3.0e6), transcendentals=0
        ),
        name=name,
    )(*args)
    return out[0] if one else out


def split(value):
    high = value.astype(bf16)
    low = (value - high.astype(f32)).astype(bf16)
    return high, low


def dot_nt(a, b):
    return lax.dot_general(a, b, (((1,), (1,)), ((), ())), preferred_element_type=f32)


def dot_nn(a, b):
    return lax.dot_general(a, b, (((1,), (0,)), ((), ())), preferred_element_type=f32)


def pack_first(
    drive_ref,
    place_ref,
    theta_ref,
    inflow_ref,
    wet_ref,
    far_ref,
    up_ref,
    down_ref,
    level_ref,
    place,
    surface,
    inflow,
    wet,
    sems,
):
    rows = drive_ref.shape[0]
    half = far_ref.shape[1]
    tiers = theta_ref.shape[0]
    base = jnp.where(lax.axis_index("lev") == 0, tiers - STEPS, 0)
    pairs = (
        (drive_ref.at[:, half : 2 * half], far_ref.at[0:rows, :]),
        (place_ref, place),
        (theta_ref.at[0 : STEPS + 1], surface),
        (inflow_ref, inflow),
        (wet_ref, wet),
        (theta_ref.at[pl.ds(base, STEPS)], level_ref),
    )
    copies = [pltpu.make_async_copy(a, b, sems.at[k]) for k, (a, b) in enumerate(pairs)]
    for copy in copies:
        copy.start()
    for copy in copies[1:5]:
        copy.wait()
    far = place[:, half : 2 * half].astype(f32)
    far_ref[rows : rows + SUBLANES, :] = jnp.broadcast_to(far, (SUBLANES, half))
    up_ref[0] = inflow[4:8, :]
    down_ref[0] = inflow[0:4, :]
    up_ref[1] = wet[4:8, :].astype(f32)
    down_ref[1] = wet[0:4, :].astype(f32)
    for k in range(STEPS + 1):
        up_ref[k + 2] = surface[k, 4:8, :]
        down_ref[k + 2] = surface[k, 0:4, :]
    copies[0].wait()
    copies[5].wait()


def pack_bulk(theta_ref, level_ref, up_ref, down_ref):
    skip = STEPS + 1
    deep = theta_ref.shape[0] - skip
    for k in range(deep):
        up_ref[k] = theta_ref[k + skip, 4:8, :]
        down_ref[k] = theta_ref[k + skip, 0:4, :]
    for j in range(STEPS):
        up_ref[deep + j] = level_ref[j, 4:8, :]
        down_ref[deep + j] = level_ref[j, 0:4, :]


def across(own, halo):
    span = own.shape[1]
    row = lax.broadcasted_iota(i32, own.shape, 0)
    first, last = row == 0, row == SUBLANES - 1
    own_less, halo_less = pltpu.roll(own, 1, 0), pltpu.roll(halo, 1, 0)
    own_more, halo_more = pltpu.roll(own, SUBLANES - 1, 0), pltpu.roll(halo, SUBLANES - 1, 0)
    own_sum = jnp.where(first, halo_less, own_less) + jnp.where(last, halo_more, own_more)
    own_sum = own_sum + (pltpu.roll(own, 1, 1) + pltpu.roll(own, span - 1, 1))
    halo_sum = jnp.where(first, own_less, halo_less) + jnp.where(last, own_more, halo_more)
    halo_sum = halo_sum + (pltpu.roll(halo, 1, 1) + pltpu.roll(halo, span - 1, 1))
    return own_sum, halo_sum


def top_level(theta_ref, before_ref, after_ref, inflow_ref, wet_ref, out_ref):
    count = STEPS + 1

    def joined(k):
        return jnp.concatenate([after_ref[k], before_ref[k]], axis=0)

    wet = (wet_ref[...].astype(f32), joined(1))
    source = tuple(flux_gain * w * s for w, s in zip(wet, (inflow_ref[...], joined(0))))
    keep = tuple(1.0 - (4 * horizontal_rate + 2 * vertical_rate) * w for w in wet)
    side = tuple(horizontal_rate * w for w in wet)
    rise = tuple(vertical_rate * w for w in wet)
    levels = [(theta_ref[k], joined(k + 2)) for k in range(count)]
    for step in range(1, STEPS + 1):
        fresh = []
        for k in range(count - step):
            sums = across(*levels[k])
            value = []
            for part in range(2):
                vertical = levels[k + 1][part]
                if k > 0:
                    vertical = vertical + levels[k - 1][part]
                new = keep[part] * levels[k][part] + side[part] * sums[part] + rise[part] * vertical
                if k == 0:
                    new = new + source[part]
                value.append(new)
            fresh.append(tuple(value))
        levels = fresh
    out_ref[...] = levels[0][0]


def ocean(
    theta_ref,
    before_ref,
    after_ref,
    before_bulk_ref,
    after_bulk_ref,
    level_ref,
    inflow_ref,
    wet_ref,
    out_ref,
    even,
    odd,
    keep,
    side,
    rise,
    source,
):
    tiers, lines, span = theta_ref.shape
    chunks = span // LANES
    places = tiers + STEPS
    skip = STEPS + 1
    lev = lax.axis_index("lev")
    lower = lev.astype(f32)
    upper = 1.0 - lower

    wet_own = wet_ref[...].astype(f32)
    wet_halo = jnp.concatenate([after_ref[1], before_ref[1]], axis=0)
    flow_halo = jnp.concatenate([after_ref[0], before_ref[0]], axis=0)
    for at, wet, flow in ((0, wet_own, inflow_ref[...]), (8, wet_halo, flow_halo)):
        rows = slice(at, at + 8)
        keep[rows, :] = 1.0 - (4 * horizontal_rate + 2 * vertical_rate) * wet
        side[rows, :] = horizontal_rate * wet
        rise[rows, :] = vertical_rate * wet
        source[rows, :] = (flux_gain * upper) * (wet * flow)

    for at in range(places):
        even[at, 0:8, :] = theta_ref[at] if at < tiers else level_ref[at - tiers]
        even[at, 8:12, :] = after_ref[at + 2] if at < skip else after_bulk_ref[at - skip]
        even[at, 12:16, :] = before_ref[at + 2] if at < skip else before_bulk_ref[at - skip]

    row = lax.broadcasted_iota(i32, (SUBLANES, LANES), 0)
    lane = lax.broadcasted_iota(i32, (SUBLANES, LANES), 1)
    first, last = row == 0, row == SUBLANES - 1
    lane_first, lane_last = lane == 0, lane == LANES - 1

    for step in range(1, STEPS + 1):
        held, fresh = (even, odd) if step % 2 else (odd, even)
        final = step == STEPS
        parts = (0,) if final else (0, 8)

        def advance(at, less, more, less_scale=None, more_scale=None, add_source=False):
            value = {
                (p, c): held[at, p : p + 8, c * LANES : (c + 1) * LANES]
                for p in (0, 8)
                for c in range(chunks)
            }
            right = {(p, c): pltpu.roll(value[p, c], 1, 1) for p in parts for c in range(chunks)}
            left = {(p, c): pltpu.roll(value[p, c], LANES - 1, 1) for p in parts for c in range(chunks)}
            for c in range(chunks):
                cols = slice(c * LANES, (c + 1) * LANES)
                own, halo = value[0, c], value[8, c]
                less_rows = {0: pltpu.roll(own, 1, 0), 8: pltpu.roll(halo, 1, 0)}
                more_rows = {0: pltpu.roll(own, 7, 0), 8: pltpu.roll(halo, 7, 0)}
                for p in parts:
                    around = jnp.where(first, less_rows[8 - p], less_rows[p])
                    around = around + jnp.where(last, more_rows[8 - p], more_rows[p])
                    along = jnp.where(lane_first, right[p, (c - 1) % chunks], right[p, c])
                    along = along + jnp.where(lane_last, left[p, (c + 1) % chunks], left[p, c])
                    rows = slice(p, p + 8)
                    a, b = held[less, rows, cols], held[more, rows, cols]
                    if less_scale is not None:
                        a = a * less_scale
                    if more_scale is not None:
                        b = b * more_scale
                    new = (
                        keep[rows, cols] * value[p, c]
                        + side[rows, cols] * (around + along)
                        + rise[rows, cols] * (a + b)
                    )
                    if add_source:
                        new = new + source[rows, cols]
                    if final:
                        out_ref[at, :, cols] = new
                    else:
                        fresh[at, rows, cols] = new

        advance(0, places - 1, 1, less_scale=lower, add_source=True)
        for at in range(1, tiers - 1):
            advance(at, at - 1, at + 1)
        advance(tiers - 1, tiers - 2, tiers, more_scale=upper)
        for j in range(STEPS - step):
            at = tiers + j + lev * step
            more = jnp.where(at == places - 1, 0, at + 1)
            advance(at, at - 1, more)


def entry_blocks(ref):
    rows, slots = ref.shape
    return [
        (slice(r, r + SUBLANES), slice(c, c + LANES))
        for r in range(0, rows, SUBLANES)
        for c in range(0, slots, LANES)
    ]


def picked(tables, keys, lanes):
    found = [jnp.zeros((SUBLANES, LANES), f32) for _ in keys]
    for r, table in enumerate(tables):
        spread = jnp.broadcast_to(table, (SUBLANES, LANES))
        found = [
            jnp.where(
                k == r, jnp.take_along_axis(spread, l, axis=1, mode="promise_in_bounds"), v
            )
            for k, l, v in zip(keys, lanes, found)
        ]
    return found


def columns(
    state_ref,
    classes_ref,
    place_ref,
    drive_ref,
    far_ref,
    link_ref,
    warmth_ref,
    sender_ref,
    share_ref,
    out_ref,
    pieces_ref,
):
    rows, count = state_ref.shape
    half = drive_ref.shape[1]
    levels = rows // 2
    width = 256

    own_drive = jnp.concatenate(split(drive_ref[...]), axis=0)
    far_drive = jnp.concatenate(split(far_ref[0:rows, :]), axis=0)
    own_place = place_ref[:, 0:half]
    far_place = far_ref[rows : rows + 1, :].astype(i32)
    link_high, link_low = split(link_ref[...])
    link_both = jnp.concatenate([link_high, link_low], axis=0)

    flux = []
    for start in range(0, count, width):
        cols = slice(start, start + width)
        target = start + lax.broadcasted_iota(i32, (width, half), 0)
        own_pick = jnp.where(target == own_place, 1.0, 0.0).astype(bf16)
        far_pick = jnp.where(target == far_place, 1.0, 0.0).astype(bf16)
        both = dot_nt(own_drive, own_pick) + dot_nt(far_drive, far_pick)
        forcing = both[0:rows] + both[rows : 2 * rows]
        x = state_ref[:, cols]
        kinds = classes_ref[:, cols]
        for k in range(CLASSES):
            high, low = split(x)
            product = dot_nn(link_both, high)
            drive = product[0:rows] + (product[rows : 2 * rows] + dot_nn(link_high, low)) + forcing
            x = x + jnp.where(kinds > k, tendency_scale * jnp.tanh(drive), 0.0)
        out_ref[:, cols] = x
        flux.append(
            surface_exchange_factor * (x[levels - 1 : levels, :] - warmth_ref[:, cols])
            + humidity_exchange_factor * x[rows - 1 : rows, :]
        )
    flux = jnp.concatenate(flux, axis=1)

    blocks = entry_blocks(sender_ref)
    lanes = [sender_ref[b] & (LANES - 1) for b in blocks]
    keys = [sender_ref[b] >> 7 for b in blocks]
    tables = [flux[:, r * LANES : (r + 1) * LANES] for r in range(count // LANES)]
    for b, v in zip(blocks, picked(tables, keys, lanes)):
        pieces_ref[b] = share_ref[b] * v


def targets(tile_ref, top_ref, top_far_ref, pieces_ref, payload_ref):
    lines, span = top_ref.shape
    surface = jnp.where(lax.axis_index("lev") == 0, top_ref[...], top_far_ref[...])
    blocks = entry_blocks(tile_ref)
    lanes = [tile_ref[b] & (LANES - 1) for b in blocks]
    keys = [tile_ref[b] >> 7 for b in blocks]
    tables = [
        surface[r : r + 1, c : c + LANES] for r in range(lines) for c in range(0, span, LANES)
    ]
    for (r, c), v in zip(blocks, picked(tables, keys, lanes)):
        part = c.start // LANES
        payload_ref[pl.ds(4 * r.start + part, SUBLANES, stride=4), :] = pieces_ref[r, c]
        payload_ref[pl.ds(4 * r.start + 2 + part, SUBLANES, stride=4), :] = v


def entry_sum(index_row, value_row, groups, order):
    entries = index_row.shape[1]
    group = order(index_row)
    hit = lax.broadcasted_iota(i32, (groups, entries), 0) == group
    high = value_row.astype(bf16).astype(f32)
    low = value_row - high
    weighted = jnp.concatenate(
        [jnp.where(hit, high, 0.0).astype(bf16), jnp.where(hit, low, 0.0).astype(bf16)], axis=0
    )
    lane = index_row & (LANES - 1)
    lane_hit = lax.broadcasted_iota(i32, (LANES, entries), 0) == lane
    return dot_nt(weighted, jnp.where(lane_hit, 1.0, 0.0).astype(bf16))


def joined_rows(ref, at):
    return jnp.concatenate([ref[at : at + 1, :], ref[at + 1 : at + 2, :]], axis=1)


def add_flux(received_ref, tile_ref, out_ref):
    entry_rows, slots = tile_ref.shape
    lines, span = out_ref.shape
    chunks = span // LANES
    groups = lines * chunks
    total = jnp.zeros((2 * groups, LANES), f32)
    for d in range(entry_rows):
        total = total + entry_sum(
            tile_ref[d : d + 1, :],
            joined_rows(received_ref, 4 * d),
            groups,
            lambda t: ((t >> 7) & (chunks - 1)) * lines + (t >> 10),
        )
    total = total[0:groups] + total[groups:]
    for c in range(chunks):
        out_ref[:, c * LANES : (c + 1) * LANES] = total[c * lines : (c + 1) * lines]


def add_warmth(received_ref, sender_ref, share_ref, out_ref):
    entry_rows, slots = sender_ref.shape
    groups = out_ref.shape[0]
    total = jnp.zeros((2 * groups, LANES), f32)
    for d in range(entry_rows):
        total = total + entry_sum(
            sender_ref[d : d + 1, :],
            joined_rows(received_ref, 4 * d + 2) * share_ref[d : d + 1, :],
            groups,
            lambda t: t >> 7,
        )
    out_ref[...] = total[0:groups] + total[groups:]


def on_device(
    air_profile_vector,
    profile_pass_kind,
    position_profile_map,
    sunlight_aerosol_drive,
    profile_link_operator,
    bottom_warmth_seen,
    intersect_sender_index,
    intersect_share,
    intersect_receiver_tile,
    marine_warmth_departure,
    earlier_bottom_inflow,
    marine_tile_indicator,
):
    rows, count = air_profile_vector.shape
    half = count // 2
    tiers, lines, span = marine_warmth_departure.shape
    entry_rows, slots = intersect_sender_index.shape
    n_dom = lax.axis_size("dom")
    n_block = lax.axis_size("comp") * n_dom
    place = position_profile_map.reshape(1, count)

    def shape(*dims):
        return jax.ShapeDtypeStruct(dims, f32)

    packed, up, down, level = call(
        pack_first,
        [
            shape(rows + SUBLANES, half),
            shape(STEPS + 3, 4, span),
            shape(STEPS + 3, 4, span),
            shape(STEPS, lines, span),
        ],
        [pl.BlockSpec(memory_space=pl.ANY)] * 5,
        (
            sunlight_aerosol_drive,
            place,
            marine_warmth_departure,
            earlier_bottom_inflow,
            marine_tile_indicator,
        ),
        "pack_first",
        1.5,
        scratch=[
            pltpu.VMEM((1, count), i32),
            pltpu.VMEM((STEPS + 1, lines, span), f32),
            pltpu.VMEM((lines, span), f32),
            pltpu.VMEM((lines, span), i32),
            pltpu.SemaphoreType.DMA((6,)),
        ],
        mib=56,
    )
    block_axes = ("comp", "dom")
    rising = [(i, i + 1) for i in range(n_block - 1)]
    falling = [(j, i) for i, j in rising]
    other = [(0, 1), (1, 0)]

    far = lax.ppermute(packed, "dom", [(i, (i + n_dom // 2) % n_dom) for i in range(n_dom)])
    level = lax.ppermute(level, "lev", other)
    before = lax.ppermute(up, block_axes, rising)
    after = lax.ppermute(down, block_axes, falling)
    later_level, before, after, far = lax.optimization_barrier((level, before, after, far))
    bulk = tiers - 1
    up_bulk, down_bulk = call(
        pack_bulk,
        [shape(bulk, 4, span), shape(bulk, 4, span)],
        [whole()] * 2,
        (marine_warmth_departure, later_level),
        "pack_bulk",
        1.0,
    )
    before_bulk = lax.ppermute(up_bulk, block_axes, rising)
    after_bulk = lax.ppermute(down_bulk, block_axes, falling)

    part = pl.BlockSpec((STEPS + 3, 4, span), lambda i: (0, 0, 0))
    top = call(
        top_level,
        shape(lines, span),
        [pl.BlockSpec((STEPS + 1, lines, span), lambda i: (0, 0, 0)), part, part, whole(), whole()],
        (marine_warmth_departure, before, after, earlier_bottom_inflow, marine_tile_indicator),
        "top_level",
        1.0,
        grid=(1,),
    )
    top_far = lax.ppermute(top, "lev", [(0, 1)])

    air_profile_updated, pieces = call(
        columns,
        [shape(rows, count), shape(entry_rows, slots)],
        [whole()] * 3 + [pl.BlockSpec((rows, half), lambda i: (0, 0))] + [whole()] * 5,
        (
            air_profile_vector,
            profile_pass_kind.reshape(1, count),
            place,
            sunlight_aerosol_drive,
            far,
            profile_link_operator,
            bottom_warmth_seen.reshape(1, count),
            intersect_sender_index,
            intersect_share,
        ),
        "columns",
        4.0,
        grid=(1,),
    )
    payload = call(
        targets,
        shape(4 * entry_rows, LANES),
        [whole()] * 4,
        (intersect_receiver_tile, top, top_far, pieces),
        "targets",
        1.0,
    )
    received = lax.all_to_all(
        payload.reshape(entry_rows, 4, LANES), "dom", split_axis=0, concat_axis=0, tiled=True
    ).reshape(4 * entry_rows, LANES)

    theta = call(
        ocean,
        shape(tiers, lines, span),
        [whole()] * 8,
        (
            marine_warmth_departure,
            before,
            after,
            before_bulk,
            after_bulk,
            level,
            earlier_bottom_inflow,
            marine_tile_indicator,
        ),
        "ocean",
        6.0,
        scratch=[pltpu.VMEM((tiers + STEPS, 16, span), f32)] * 2 + [pltpu.VMEM((16, span), f32)] * 4,
    )

    partial_flux = call(
        add_flux,
        shape(lines, span),
        [whole()] * 2,
        (received, intersect_receiver_tile),
        "add_flux",
        2.0,
    )
    marine_warming_rate = partial_flux + lax.ppermute(partial_flux, "lev", other)
    air_bottom_warmth = call(
        add_warmth,
        shape(count // LANES, LANES),
        [whole()] * 3,
        (received, intersect_sender_index, intersect_share),
        "add_warmth",
        2.0,
    ).reshape(count)
    return (air_profile_updated, theta, marine_warming_rate, air_bottom_warmth)


def solution(mesh):
    placed = (
        P(None, ("comp", "dom", "lev")),
        P(("comp", "dom", "lev")),
        P(("comp", "dom", "lev")),
        P(None, ("comp", "dom", "lev")),
        P(),
        P(("comp", "dom", "lev")),
        P(("comp", "dom", "lev"), None),
        P(("comp", "dom", "lev"), None),
        P(("comp", "dom", "lev"), None),
        P("lev", ("comp", "dom"), None),
        P(("comp", "dom"), None),
        P(("comp", "dom"), None),
    )
    return jax.shard_map(
        on_device,
        mesh=mesh,
        in_specs=placed,
        out_specs=(
            P(None, ("comp", "dom", "lev")),
            P("lev", ("comp", "dom"), None),
            P(("comp", "dom"), None),
            P(("comp", "dom", "lev")),
        ),
        check_vma=False,
    )
```

```python
import jax
import jax.numpy as jnp
from jax import lax
from jax.experimental import pallas as pl
from jax.experimental.pallas import tpu as pltpu
from jax.sharding import PartitionSpec as P

STEPS = 4
CLASSES = 3
LANES = 128
SUBLANES = 8

surface_exchange_factor = 0.8
humidity_exchange_factor = 0.5
tendency_scale = 0.5
horizontal_rate = 0.15
vertical_rate = 0.1
flux_gain = 0.5

f32 = jnp.float32
bf16 = jnp.bfloat16
i32 = jnp.int32


def whole():
    return pl.BlockSpec(memory_space=pltpu.VMEM)


def call(body, out_shapes, specs, args, name, microseconds, scratch=(), mib=32, grid=()):
    one = not isinstance(out_shapes, (list, tuple))
    shapes = [out_shapes] if one else list(out_shapes)
    out = pl.pallas_call(
        body,
        out_shape=shapes,
        grid=grid,
        in_specs=specs,
        out_specs=[whole() for _ in shapes],
        scratch_shapes=list(scratch),
        compiler_params=pltpu.CompilerParams(vmem_limit_bytes=mib * 1024 * 1024),
        cost_estimate=pl.CostEstimate(
            flops=int(microseconds * 1.0e9), bytes_accessed=int(microseconds * 3.0e6), transcendentals=0
        ),
        name=name,
    )(*args)
    return out[0] if one else out


def split(value):
    high = value.astype(bf16)
    low = (value - high.astype(f32)).astype(bf16)
    return high, low


def dot_nt(a, b):
    return lax.dot_general(a, b, (((1,), (1,)), ((), ())), preferred_element_type=f32)


def dot_nn(a, b):
    return lax.dot_general(a, b, (((1,), (0,)), ((), ())), preferred_element_type=f32)


def is_even():
    return lax.rem(lax.axis_index("dom"), 2) == 0


def edges(even, plane):
    low, high = plane[0:4, :], plane[4:8, :]
    return jnp.where(even, high, low), jnp.where(even, low, high)


def halo_rows(even, mate, other):
    return jnp.concatenate([jnp.where(even, mate, other), jnp.where(even, other, mate)], axis=0)


def pack_first(
    drive_ref,
    place_ref,
    theta_ref,
    inflow_ref,
    wet_ref,
    far_ref,
    mate_ref,
    next_ref,
    level_ref,
    place,
    surface,
    inflow,
    wet,
    sems,
):
    rows = drive_ref.shape[0]
    half = far_ref.shape[1]
    tiers = theta_ref.shape[0]
    base = jnp.where(lax.axis_index("lev") == 0, tiers - STEPS, 0)
    pairs = (
        (drive_ref.at[:, half : 2 * half], far_ref.at[0:rows, :]),
        (place_ref, place),
        (theta_ref.at[0 : STEPS + 1], surface),
        (inflow_ref, inflow),
        (wet_ref, wet),
        (theta_ref.at[pl.ds(base, STEPS)], level_ref),
    )
    copies = [pltpu.make_async_copy(a, b, sems.at[k]) for k, (a, b) in enumerate(pairs)]
    for copy in copies:
        copy.start()
    for copy in copies[1:5]:
        copy.wait()
    far = place[:, half : 2 * half].astype(f32)
    far_ref[rows : rows + SUBLANES, :] = jnp.broadcast_to(far, (SUBLANES, half))
    even = is_even()
    mate_ref[0], next_ref[0] = edges(even, inflow[...])
    mate_ref[1], next_ref[1] = edges(even, wet[...].astype(f32))
    for k in range(STEPS + 1):
        mate_ref[k + 2], next_ref[k + 2] = edges(even, surface[k])
    copies[0].wait()
    copies[5].wait()


def pack_bulk(theta_ref, level_ref, mate_ref, next_ref):
    even = is_even()
    skip = STEPS + 1
    deep = theta_ref.shape[0] - skip
    for k in range(deep):
        mate_ref[k], next_ref[k] = edges(even, theta_ref[k + skip])
    for j in range(STEPS):
        mate_ref[deep + j], next_ref[deep + j] = edges(even, level_ref[j])


def across(own, halo):
    span = own.shape[1]
    row = lax.broadcasted_iota(i32, own.shape, 0)
    first, last = row == 0, row == SUBLANES - 1
    own_less, halo_less = pltpu.roll(own, 1, 0), pltpu.roll(halo, 1, 0)
    own_more, halo_more = pltpu.roll(own, SUBLANES - 1, 0), pltpu.roll(halo, SUBLANES - 1, 0)
    own_sum = jnp.where(first, halo_less, own_less) + jnp.where(last, halo_more, own_more)
    own_sum = own_sum + (pltpu.roll(own, 1, 1) + pltpu.roll(own, span - 1, 1))
    halo_sum = jnp.where(first, own_less, halo_less) + jnp.where(last, own_more, halo_more)
    halo_sum = halo_sum + (pltpu.roll(halo, 1, 1) + pltpu.roll(halo, span - 1, 1))
    return own_sum, halo_sum


def top_level(theta_ref, mate_ref, next_ref, inflow_ref, wet_ref, out_ref):
    count = STEPS + 1
    even = is_even()

    def joined(k):
        return halo_rows(even, mate_ref[k], next_ref[k])

    wet = (wet_ref[...].astype(f32), joined(1))
    source = tuple(flux_gain * w * s for w, s in zip(wet, (inflow_ref[...], joined(0))))
    keep = tuple(1.0 - (4 * horizontal_rate + 2 * vertical_rate) * w for w in wet)
    side = tuple(horizontal_rate * w for w in wet)
    rise = tuple(vertical_rate * w for w in wet)
    levels = [(theta_ref[k], joined(k + 2)) for k in range(count)]
    for step in range(1, STEPS + 1):
        fresh = []
        for k in range(count - step):
            sums = across(*levels[k])
            value = []
            for part in range(2):
                vertical = levels[k + 1][part]
                if k > 0:
                    vertical = vertical + levels[k - 1][part]
                new = keep[part] * levels[k][part] + side[part] * sums[part] + rise[part] * vertical
                if k == 0:
                    new = new + source[part]
                value.append(new)
            fresh.append(tuple(value))
        levels = fresh
    out_ref[...] = levels[0][0]


def ocean(
    theta_ref,
    mate_ref,
    next_ref,
    mate_bulk_ref,
    next_bulk_ref,
    level_ref,
    inflow_ref,
    wet_ref,
    out_ref,
    even,
    odd,
    keep,
    side,
    rise,
    source,
):
    tiers, lines, span = theta_ref.shape
    chunks = span // LANES
    places = tiers + STEPS
    skip = STEPS + 1
    lev = lax.axis_index("lev")
    lower = lev.astype(f32)
    upper = 1.0 - lower

    wet_own = wet_ref[...].astype(f32)
    even_block = is_even()
    wet_halo = halo_rows(even_block, mate_ref[1], next_ref[1])
    flow_halo = halo_rows(even_block, mate_ref[0], next_ref[0])
    for at, wet, flow in ((0, wet_own, inflow_ref[...]), (8, wet_halo, flow_halo)):
        rows = slice(at, at + 8)
        keep[rows, :] = 1.0 - (4 * horizontal_rate + 2 * vertical_rate) * wet
        side[rows, :] = horizontal_rate * wet
        rise[rows, :] = vertical_rate * wet
        source[rows, :] = (flux_gain * upper) * (wet * flow)

    for at in range(places):
        even[at, 0:8, :] = theta_ref[at] if at < tiers else level_ref[at - tiers]
        if at < skip:
            mate, other = mate_ref[at + 2], next_ref[at + 2]
        else:
            mate, other = mate_bulk_ref[at - skip], next_bulk_ref[at - skip]
        even[at, 8:12, :] = jnp.where(even_block, mate, other)
        even[at, 12:16, :] = jnp.where(even_block, other, mate)

    row = lax.broadcasted_iota(i32, (SUBLANES, LANES), 0)
    lane = lax.broadcasted_iota(i32, (SUBLANES, LANES), 1)
    first, last = row == 0, row == SUBLANES - 1
    lane_first, lane_last = lane == 0, lane == LANES - 1

    for step in range(1, STEPS + 1):
        held, fresh = (even, odd) if step % 2 else (odd, even)
        final = step == STEPS
        parts = (0,) if final else (0, 8)

        def advance(at, less, more, less_scale=None, more_scale=None, add_source=False):
            value = {
                (p, c): held[at, p : p + 8, c * LANES : (c + 1) * LANES]
                for p in (0, 8)
                for c in range(chunks)
            }
            right = {(p, c): pltpu.roll(value[p, c], 1, 1) for p in parts for c in range(chunks)}
            left = {(p, c): pltpu.roll(value[p, c], LANES - 1, 1) for p in parts for c in range(chunks)}
            for c in range(chunks):
                cols = slice(c * LANES, (c + 1) * LANES)
                own, halo = value[0, c], value[8, c]
                less_rows = {0: pltpu.roll(own, 1, 0), 8: pltpu.roll(halo, 1, 0)}
                more_rows = {0: pltpu.roll(own, 7, 0), 8: pltpu.roll(halo, 7, 0)}
                for p in parts:
                    around = jnp.where(first, less_rows[8 - p], less_rows[p])
                    around = around + jnp.where(last, more_rows[8 - p], more_rows[p])
                    along = jnp.where(lane_first, right[p, (c - 1) % chunks], right[p, c])
                    along = along + jnp.where(lane_last, left[p, (c + 1) % chunks], left[p, c])
                    rows = slice(p, p + 8)
                    a, b = held[less, rows, cols], held[more, rows, cols]
                    if less_scale is not None:
                        a = a * less_scale
                    if more_scale is not None:
                        b = b * more_scale
                    new = (
                        keep[rows, cols] * value[p, c]
                        + side[rows, cols] * (around + along)
                        + rise[rows, cols] * (a + b)
                    )
                    if add_source:
                        new = new + source[rows, cols]
                    if final:
                        out_ref[at, :, cols] = new
                    else:
                        fresh[at, rows, cols] = new

        advance(0, places - 1, 1, less_scale=lower, add_source=True)
        for at in range(1, tiers - 1):
            advance(at, at - 1, at + 1)
        advance(tiers - 1, tiers - 2, tiers, more_scale=upper)
        for j in range(STEPS - step):
            at = tiers + j + lev * step
            more = jnp.where(at == places - 1, 0, at + 1)
            advance(at, at - 1, more)


def entry_blocks(ref):
    rows, slots = ref.shape
    return [
        (slice(r, r + SUBLANES), slice(c, c + LANES))
        for r in range(0, rows, SUBLANES)
        for c in range(0, slots, LANES)
    ]


def picked(tables, keys, lanes):
    found = [jnp.zeros((SUBLANES, LANES), f32) for _ in keys]
    for r, table in enumerate(tables):
        spread = jnp.broadcast_to(table, (SUBLANES, LANES))
        found = [
            jnp.where(
                k == r, jnp.take_along_axis(spread, l, axis=1, mode="promise_in_bounds"), v
            )
            for k, l, v in zip(keys, lanes, found)
        ]
    return found


def columns(
    state_ref,
    classes_ref,
    place_ref,
    drive_ref,
    far_ref,
    link_ref,
    warmth_ref,
    sender_ref,
    share_ref,
    out_ref,
    pieces_ref,
):
    rows, count = state_ref.shape
    half = drive_ref.shape[1]
    levels = rows // 2
    width = 256

    own_drive = jnp.concatenate(split(drive_ref[...]), axis=0)
    far_drive = jnp.concatenate(split(far_ref[0:rows, :]), axis=0)
    own_place = place_ref[:, 0:half]
    far_place = far_ref[rows : rows + 1, :].astype(i32)
    link_high, link_low = split(link_ref[...])
    link_both = jnp.concatenate([link_high, link_low], axis=0)

    flux = []
    for start in range(0, count, width):
        cols = slice(start, start + width)
        target = start + lax.broadcasted_iota(i32, (width, half), 0)
        own_pick = jnp.where(target == own_place, 1.0, 0.0).astype(bf16)
        far_pick = jnp.where(target == far_place, 1.0, 0.0).astype(bf16)
        both = dot_nt(own_drive, own_pick) + dot_nt(far_drive, far_pick)
        forcing = both[0:rows] + both[rows : 2 * rows]
        x = state_ref[:, cols]
        kinds = classes_ref[:, cols]
        for k in range(CLASSES):
            high, low = split(x)
            product = dot_nn(link_both, high)
            drive = product[0:rows] + (product[rows : 2 * rows] + dot_nn(link_high, low)) + forcing
            x = x + jnp.where(kinds > k, tendency_scale * jnp.tanh(drive), 0.0)
        out_ref[:, cols] = x
        flux.append(
            surface_exchange_factor * (x[levels - 1 : levels, :] - warmth_ref[:, cols])
            + humidity_exchange_factor * x[rows - 1 : rows, :]
        )
    flux = jnp.concatenate(flux, axis=1)

    blocks = entry_blocks(sender_ref)
    lanes = [sender_ref[b] & (LANES - 1) for b in blocks]
    keys = [sender_ref[b] >> 7 for b in blocks]
    tables = [flux[:, r * LANES : (r + 1) * LANES] for r in range(count // LANES)]
    for b, v in zip(blocks, picked(tables, keys, lanes)):
        pieces_ref[b] = share_ref[b] * v


def targets(tile_ref, top_ref, top_far_ref, pieces_ref, payload_ref):
    lines, span = top_ref.shape
    surface = jnp.where(lax.axis_index("lev") == 0, top_ref[...], top_far_ref[...])
    blocks = entry_blocks(tile_ref)
    lanes = [tile_ref[b] & (LANES - 1) for b in blocks]
    keys = [tile_ref[b] >> 7 for b in blocks]
    tables = [
        surface[r : r + 1, c : c + LANES] for r in range(lines) for c in range(0, span, LANES)
    ]
    for (r, c), v in zip(blocks, picked(tables, keys, lanes)):
        part = c.start // LANES
        payload_ref[pl.ds(4 * r.start + part, SUBLANES, stride=4), :] = pieces_ref[r, c]
        payload_ref[pl.ds(4 * r.start + 2 + part, SUBLANES, stride=4), :] = v


def entry_sum(index_row, value_row, groups, order):
    entries = index_row.shape[1]
    group = order(index_row)
    hit = lax.broadcasted_iota(i32, (groups, entries), 0) == group
    high = value_row.astype(bf16).astype(f32)
    low = value_row - high
    weighted = jnp.concatenate(
        [jnp.where(hit, high, 0.0).astype(bf16), jnp.where(hit, low, 0.0).astype(bf16)], axis=0
    )
    lane = index_row & (LANES - 1)
    lane_hit = lax.broadcasted_iota(i32, (LANES, entries), 0) == lane
    return dot_nt(weighted, jnp.where(lane_hit, 1.0, 0.0).astype(bf16))


def joined_rows(ref, at):
    return jnp.concatenate([ref[at : at + 1, :], ref[at + 1 : at + 2, :]], axis=1)


def add_flux(received_ref, tile_ref, out_ref):
    entry_rows, slots = tile_ref.shape
    lines, span = out_ref.shape
    chunks = span // LANES
    groups = lines * chunks
    total = jnp.zeros((2 * groups, LANES), f32)
    for d in range(entry_rows):
        total = total + entry_sum(
            tile_ref[d : d + 1, :],
            joined_rows(received_ref, 4 * d),
            groups,
            lambda t: ((t >> 7) & (chunks - 1)) * lines + (t >> 10),
        )
    total = total[0:groups] + total[groups:]
    for c in range(chunks):
        out_ref[:, c * LANES : (c + 1) * LANES] = total[c * lines : (c + 1) * lines]


def add_warmth(received_ref, sender_ref, share_ref, out_ref):
    entry_rows, slots = sender_ref.shape
    groups = out_ref.shape[0]
    total = jnp.zeros((2 * groups, LANES), f32)
    for d in range(entry_rows):
        total = total + entry_sum(
            sender_ref[d : d + 1, :],
            joined_rows(received_ref, 4 * d + 2) * share_ref[d : d + 1, :],
            groups,
            lambda t: t >> 7,
        )
    out_ref[...] = total[0:groups] + total[groups:]


def on_device(
    air_profile_vector,
    profile_pass_kind,
    position_profile_map,
    sunlight_aerosol_drive,
    profile_link_operator,
    bottom_warmth_seen,
    intersect_sender_index,
    intersect_share,
    intersect_receiver_tile,
    marine_warmth_departure,
    earlier_bottom_inflow,
    marine_tile_indicator,
):
    rows, count = air_profile_vector.shape
    half = count // 2
    tiers, lines, span = marine_warmth_departure.shape
    entry_rows, slots = intersect_sender_index.shape
    n_dom = lax.axis_size("dom")
    n_block = lax.axis_size("comp") * n_dom
    place = position_profile_map.reshape(1, count)

    def shape(*dims):
        return jax.ShapeDtypeStruct(dims, f32)

    packed, mate, follow, level = call(
        pack_first,
        [
            shape(rows + SUBLANES, half),
            shape(STEPS + 3, 4, span),
            shape(STEPS + 3, 4, span),
            shape(STEPS, lines, span),
        ],
        [pl.BlockSpec(memory_space=pl.ANY)] * 5,
        (
            sunlight_aerosol_drive,
            place,
            marine_warmth_departure,
            earlier_bottom_inflow,
            marine_tile_indicator,
        ),
        "pack_first",
        1.5,
        scratch=[
            pltpu.VMEM((1, count), i32),
            pltpu.VMEM((STEPS + 1, lines, span), f32),
            pltpu.VMEM((lines, span), f32),
            pltpu.VMEM((lines, span), i32),
            pltpu.SemaphoreType.DMA((6,)),
        ],
        mib=56,
    )
    block_axes = ("comp", "dom")
    mates = [(i, i ^ 1) for i in range(n_block)]
    nexts = [(i, i + 1) for i in range(1, n_block - 1, 2)]
    nexts = nexts + [(j, i) for i, j in nexts]
    other = [(0, 1), (1, 0)]

    far = lax.ppermute(packed, "dom", [(i, (i + n_dom // 2) % n_dom) for i in range(n_dom)])
    level = lax.ppermute(level, "lev", other)
    mate = lax.ppermute(mate, block_axes, mates)
    follow = lax.ppermute(follow, block_axes, nexts)
    later_level = level
    bulk = tiers - 1
    mate_bulk, follow_bulk = call(
        pack_bulk,
        [shape(bulk, 4, span), shape(bulk, 4, span)],
        [whole()] * 2,
        (marine_warmth_departure, later_level),
        "pack_bulk",
        1.0,
    )
    mate_bulk = lax.ppermute(mate_bulk, block_axes, mates)
    follow_bulk = lax.ppermute(follow_bulk, block_axes, nexts)

    air_profile_updated, pieces = call(
        columns,
        [shape(rows, count), shape(entry_rows, slots)],
        [whole()] * 3 + [pl.BlockSpec((rows, half), lambda i: (0, 0))] + [whole()] * 5,
        (
            air_profile_vector,
            profile_pass_kind.reshape(1, count),
            place,
            sunlight_aerosol_drive,
            far,
            profile_link_operator,
            bottom_warmth_seen.reshape(1, count),
            intersect_sender_index,
            intersect_share,
        ),
        "columns",
        4.0,
        grid=(1,),
    )
    mate, follow, pieces = lax.optimization_barrier((mate, follow, pieces))
    part = pl.BlockSpec((STEPS + 3, 4, span), lambda i: (0, 0, 0))
    top = call(
        top_level,
        shape(lines, span),
        [pl.BlockSpec((STEPS + 1, lines, span), lambda i: (0, 0, 0)), part, part, whole(), whole()],
        (marine_warmth_departure, mate, follow, earlier_bottom_inflow, marine_tile_indicator),
        "top_level",
        1.0,
        grid=(1,),
    )
    top_far = lax.ppermute(top, "lev", [(0, 1)])

    payload = call(
        targets,
        shape(4 * entry_rows, LANES),
        [whole()] * 4,
        (intersect_receiver_tile, top, top_far, pieces),
        "targets",
        1.0,
    )
    received = lax.all_to_all(
        payload.reshape(entry_rows, 4, LANES), "dom", split_axis=0, concat_axis=0, tiled=True
    ).reshape(4 * entry_rows, LANES)

    partial_flux = call(
        add_flux,
        shape(lines, span),
        [whole()] * 2,
        (received, intersect_receiver_tile),
        "add_flux",
        2.0,
    )
    late_level, partial_flux = lax.optimization_barrier((level, partial_flux))
    theta = call(
        ocean,
        shape(tiers, lines, span),
        [whole()] * 8,
        (
            marine_warmth_departure,
            mate,
            follow,
            mate_bulk,
            follow_bulk,
            late_level,
            earlier_bottom_inflow,
            marine_tile_indicator,
        ),
        "ocean",
        6.0,
        scratch=[pltpu.VMEM((tiers + STEPS, 16, span), f32)] * 2 + [pltpu.VMEM((16, span), f32)] * 4,
    )

    other_flux = lax.ppermute(partial_flux, "lev", other)
    theta, other_flux = lax.optimization_barrier((theta, other_flux))
    marine_warming_rate = partial_flux + other_flux
    air_bottom_warmth = call(
        add_warmth,
        shape(count // LANES, LANES),
        [whole()] * 3,
        (received, intersect_sender_index, intersect_share),
        "add_warmth",
        2.0,
    ).reshape(count)
    return (air_profile_updated, theta, marine_warming_rate, air_bottom_warmth)


def solution(mesh):
    placed = (
        P(None, ("comp", "dom", "lev")),
        P(("comp", "dom", "lev")),
        P(("comp", "dom", "lev")),
        P(None, ("comp", "dom", "lev")),
        P(),
        P(("comp", "dom", "lev")),
        P(("comp", "dom", "lev"), None),
        P(("comp", "dom", "lev"), None),
        P(("comp", "dom", "lev"), None),
        P("lev", ("comp", "dom"), None),
        P(("comp", "dom"), None),
        P(("comp", "dom"), None),
    )
    return jax.shard_map(
        on_device,
        mesh=mesh,
        in_specs=placed,
        out_specs=(
            P(None, ("comp", "dom", "lev")),
            P("lev", ("comp", "dom"), None),
            P(("comp", "dom"), None),
            P(("comp", "dom", "lev")),
        ),
        check_vma=False,
    )
```

```python
import jax
import jax.numpy as jnp
from jax import lax
from jax.experimental import pallas as pl
from jax.experimental.pallas import tpu as pltpu
from jax.sharding import PartitionSpec as P

STEPS = 4
CLASSES = 3
LANES = 128
SUBLANES = 8

surface_exchange_factor = 0.8
humidity_exchange_factor = 0.5
tendency_scale = 0.5
horizontal_rate = 0.15
vertical_rate = 0.1
flux_gain = 0.5

f32 = jnp.float32
bf16 = jnp.bfloat16
i32 = jnp.int32


def whole():
    return pl.BlockSpec(memory_space=pltpu.VMEM)


def call(body, out_shapes, specs, args, name, microseconds, scratch=(), mib=32, grid=(), out_specs=None):
    one = not isinstance(out_shapes, (list, tuple))
    shapes = [out_shapes] if one else list(out_shapes)
    out = pl.pallas_call(
        body,
        out_shape=shapes,
        grid=grid,
        in_specs=specs,
        out_specs=out_specs or [whole() for _ in shapes],
        scratch_shapes=list(scratch),
        compiler_params=pltpu.CompilerParams(vmem_limit_bytes=mib * 1024 * 1024),
        cost_estimate=pl.CostEstimate(
            flops=int(microseconds * 1.0e9), bytes_accessed=int(microseconds * 3.0e6), transcendentals=0
        ),
        name=name,
    )(*args)
    return out[0] if one else out


def split(value):
    high = value.astype(bf16)
    low = (value - high.astype(f32)).astype(bf16)
    return high, low


def dot_nt(a, b):
    return lax.dot_general(a, b, (((1,), (1,)), ((), ())), preferred_element_type=f32)


def dot_nn(a, b):
    return lax.dot_general(a, b, (((1,), (0,)), ((), ())), preferred_element_type=f32)


def is_even():
    return lax.rem(lax.axis_index("dom"), 2) == 0


def edges(even, plane):
    low, high = plane[0:4, :], plane[4:8, :]
    return jnp.where(even, high, low), jnp.where(even, low, high)


def halo_rows(even, mate, other):
    return jnp.concatenate([jnp.where(even, mate, other), jnp.where(even, other, mate)], axis=0)


def pack_first(
    drive_ref,
    place_ref,
    theta_ref,
    inflow_ref,
    wet_ref,
    far_ref,
    mate_ref,
    next_ref,
    level_ref,
    place,
    surface,
    inflow,
    wet,
    far_rows,
    sems,
):
    rows = drive_ref.shape[0]
    half = far_ref.shape[1]
    tiers = theta_ref.shape[0]
    base = jnp.where(lax.axis_index("lev") == 0, tiers - STEPS, 0)
    pairs = (
        (drive_ref.at[:, half : 2 * half], far_ref.at[0:rows, :]),
        (place_ref, place),
        (theta_ref.at[0 : STEPS + 1], surface),
        (inflow_ref, inflow),
        (wet_ref, wet),
        (theta_ref.at[pl.ds(base, STEPS)], level_ref),
    )
    copies = [pltpu.make_async_copy(a, b, sems.at[k]) for k, (a, b) in enumerate(pairs)]
    for copy in copies:
        copy.start()
    for copy in copies[1:5]:
        copy.wait()
    far = place[:, half : 2 * half].astype(f32)
    far_rows[...] = jnp.broadcast_to(far, (SUBLANES, half))
    last = pltpu.make_async_copy(far_rows, far_ref.at[rows : rows + SUBLANES, :], sems.at[len(pairs)])
    last.start()
    even = is_even()
    mate_ref[0], next_ref[0] = edges(even, inflow[...])
    mate_ref[1], next_ref[1] = edges(even, wet[...].astype(f32))
    for k in range(STEPS + 1):
        mate_ref[k + 2], next_ref[k + 2] = edges(even, surface[k])
    copies[0].wait()
    copies[5].wait()
    last.wait()


def pack_bulk(theta_ref, level_ref, mate_ref, next_ref):
    even = is_even()
    skip = STEPS + 1
    deep = theta_ref.shape[0] - skip
    for k in range(deep):
        mate_ref[k], next_ref[k] = edges(even, theta_ref[k + skip])
    for j in range(STEPS):
        mate_ref[deep + j], next_ref[deep + j] = edges(even, level_ref[j])


def across(own, halo):
    span = own.shape[1]
    row = lax.broadcasted_iota(i32, own.shape, 0)
    first, last = row == 0, row == SUBLANES - 1
    own_less, halo_less = pltpu.roll(own, 1, 0), pltpu.roll(halo, 1, 0)
    own_more, halo_more = pltpu.roll(own, SUBLANES - 1, 0), pltpu.roll(halo, SUBLANES - 1, 0)
    own_sum = jnp.where(first, halo_less, own_less) + jnp.where(last, halo_more, own_more)
    own_sum = own_sum + (pltpu.roll(own, 1, 1) + pltpu.roll(own, span - 1, 1))
    halo_sum = jnp.where(first, own_less, halo_less) + jnp.where(last, own_more, halo_more)
    halo_sum = halo_sum + (pltpu.roll(halo, 1, 1) + pltpu.roll(halo, span - 1, 1))
    return own_sum, halo_sum


def top_level(theta_ref, mate_ref, next_ref, inflow_ref, wet_ref, out_ref):
    count = STEPS + 1
    even = is_even()

    def joined(k):
        return halo_rows(even, mate_ref[k], next_ref[k])

    wet = (wet_ref[...].astype(f32), joined(1))
    source = tuple(flux_gain * w * s for w, s in zip(wet, (inflow_ref[...], joined(0))))
    keep = tuple(1.0 - (4 * horizontal_rate + 2 * vertical_rate) * w for w in wet)
    side = tuple(horizontal_rate * w for w in wet)
    rise = tuple(vertical_rate * w for w in wet)
    levels = [(theta_ref[k], joined(k + 2)) for k in range(count)]
    for step in range(1, STEPS + 1):
        fresh = []
        for k in range(count - step):
            sums = across(*levels[k])
            value = []
            for part in range(2):
                vertical = levels[k + 1][part]
                if k > 0:
                    vertical = vertical + levels[k - 1][part]
                new = keep[part] * levels[k][part] + side[part] * sums[part] + rise[part] * vertical
                if k == 0:
                    new = new + source[part]
                value.append(new)
            fresh.append(tuple(value))
        levels = fresh
    out_ref[...] = levels[0][0]


def ocean(
    theta_ref,
    mate_ref,
    next_ref,
    mate_bulk_ref,
    next_bulk_ref,
    level_ref,
    inflow_ref,
    wet_ref,
    out_ref,
    even,
    odd,
    keep,
    side,
    rise,
    source,
):
    tiers, lines, span = theta_ref.shape
    chunks = span // LANES
    places = tiers + STEPS
    skip = STEPS + 1
    lev = lax.axis_index("lev")
    lower = lev.astype(f32)
    upper = 1.0 - lower

    wet_own = wet_ref[...].astype(f32)
    even_block = is_even()
    wet_halo = halo_rows(even_block, mate_ref[1], next_ref[1])
    flow_halo = halo_rows(even_block, mate_ref[0], next_ref[0])
    for at, wet, flow in ((0, wet_own, inflow_ref[...]), (8, wet_halo, flow_halo)):
        rows = slice(at, at + 8)
        keep[rows, :] = 1.0 - (4 * horizontal_rate + 2 * vertical_rate) * wet
        side[rows, :] = horizontal_rate * wet
        rise[rows, :] = vertical_rate * wet
        source[rows, :] = (flux_gain * upper) * (wet * flow)

    for at in range(places):
        even[at, 0:8, :] = theta_ref[at] if at < tiers else level_ref[at - tiers]
        if at < skip:
            mate, other = mate_ref[at + 2], next_ref[at + 2]
        else:
            mate, other = mate_bulk_ref[at - skip], next_bulk_ref[at - skip]
        even[at, 8:12, :] = jnp.where(even_block, mate, other)
        even[at, 12:16, :] = jnp.where(even_block, other, mate)

    row = lax.broadcasted_iota(i32, (SUBLANES, LANES), 0)
    lane = lax.broadcasted_iota(i32, (SUBLANES, LANES), 1)
    first, last = row == 0, row == SUBLANES - 1
    lane_first, lane_last = lane == 0, lane == LANES - 1

    for step in range(1, STEPS + 1):
        held, fresh = (even, odd) if step % 2 else (odd, even)
        final = step == STEPS
        parts = (0,) if final else (0, 8)

        def advance(at, less, more, less_scale=None, more_scale=None, add_source=False):
            value = {
                (p, c): held[at, p : p + 8, c * LANES : (c + 1) * LANES]
                for p in (0, 8)
                for c in range(chunks)
            }
            right = {(p, c): pltpu.roll(value[p, c], 1, 1) for p in parts for c in range(chunks)}
            left = {(p, c): pltpu.roll(value[p, c], LANES - 1, 1) for p in parts for c in range(chunks)}
            for c in range(chunks):
                cols = slice(c * LANES, (c + 1) * LANES)
                own, halo = value[0, c], value[8, c]
                less_rows = {0: pltpu.roll(own, 1, 0), 8: pltpu.roll(halo, 1, 0)}
                more_rows = {0: pltpu.roll(own, 7, 0), 8: pltpu.roll(halo, 7, 0)}
                for p in parts:
                    around = jnp.where(first, less_rows[8 - p], less_rows[p])
                    around = around + jnp.where(last, more_rows[8 - p], more_rows[p])
                    along = jnp.where(lane_first, right[p, (c - 1) % chunks], right[p, c])
                    along = along + jnp.where(lane_last, left[p, (c + 1) % chunks], left[p, c])
                    rows = slice(p, p + 8)
                    a, b = held[less, rows, cols], held[more, rows, cols]
                    if less_scale is not None:
                        a = a * less_scale
                    if more_scale is not None:
                        b = b * more_scale
                    new = (
                        keep[rows, cols] * value[p, c]
                        + side[rows, cols] * (around + along)
                        + rise[rows, cols] * (a + b)
                    )
                    if add_source:
                        new = new + source[rows, cols]
                    if final:
                        out_ref[at, :, cols] = new
                    else:
                        fresh[at, rows, cols] = new

        advance(0, places - 1, 1, less_scale=lower, add_source=True)
        for at in range(1, tiers - 1):
            advance(at, at - 1, at + 1)
        advance(tiers - 1, tiers - 2, tiers, more_scale=upper)
        for j in range(STEPS - step):
            at = tiers + j + lev * step
            more = jnp.where(at == places - 1, 0, at + 1)
            advance(at, at - 1, more)


def entry_blocks(ref):
    rows, slots = ref.shape
    return [
        (slice(r, r + SUBLANES), slice(c, c + LANES))
        for r in range(0, rows, SUBLANES)
        for c in range(0, slots, LANES)
    ]


def picked(tables, keys, lanes):
    found = [jnp.zeros((SUBLANES, LANES), f32) for _ in keys]
    for r, table in enumerate(tables):
        spread = jnp.broadcast_to(table, (SUBLANES, LANES))
        found = [
            jnp.where(
                k == r, jnp.take_along_axis(spread, l, axis=1, mode="promise_in_bounds"), v
            )
            for k, l, v in zip(keys, lanes, found)
        ]
    return found


def columns(
    state_ref,
    classes_ref,
    place_ref,
    drive_ref,
    far_ref,
    link_ref,
    warmth_ref,
    sender_ref,
    share_ref,
    out_ref,
    pieces_ref,
):
    rows, count = state_ref.shape
    half = drive_ref.shape[1]
    levels = rows // 2
    width = 256

    own_drive = jnp.concatenate(split(drive_ref[...]), axis=0)
    far_drive = jnp.concatenate(split(far_ref[0:rows, :]), axis=0)
    own_place = place_ref[:, 0:half]
    far_place = far_ref[rows : rows + 1, :].astype(i32)
    link_high, link_low = split(link_ref[...])
    link_both = jnp.concatenate([link_high, link_low], axis=0)

    flux = []
    for start in range(0, count, width):
        cols = slice(start, start + width)
        target = start + lax.broadcasted_iota(i32, (width, half), 0)
        own_pick = jnp.where(target == own_place, 1.0, 0.0).astype(bf16)
        far_pick = jnp.where(target == far_place, 1.0, 0.0).astype(bf16)
        both = dot_nt(own_drive, own_pick) + dot_nt(far_drive, far_pick)
        forcing = both[0:rows] + both[rows : 2 * rows]
        x = state_ref[:, cols]
        kinds = classes_ref[:, cols]
        for k in range(CLASSES):
            high, low = split(x)
            product = dot_nn(link_both, high)
            drive = product[0:rows] + (product[rows : 2 * rows] + dot_nn(link_high, low)) + forcing
            x = x + jnp.where(kinds > k, tendency_scale * jnp.tanh(drive), 0.0)
        out_ref[:, cols] = x
        flux.append(
            surface_exchange_factor * (x[levels - 1 : levels, :] - warmth_ref[:, cols])
            + humidity_exchange_factor * x[rows - 1 : rows, :]
        )
    flux = jnp.concatenate(flux, axis=1)

    blocks = entry_blocks(sender_ref)
    lanes = [sender_ref[b] & (LANES - 1) for b in blocks]
    keys = [sender_ref[b] >> 7 for b in blocks]
    tables = [flux[:, r * LANES : (r + 1) * LANES] for r in range(count // LANES)]
    for b, v in zip(blocks, picked(tables, keys, lanes)):
        pieces_ref[b] = share_ref[b] * v


def targets(tile_ref, top_ref, top_far_ref, pieces_ref, payload_ref):
    lines, span = top_ref.shape
    surface = jnp.where(lax.axis_index("lev") == 0, top_ref[...], top_far_ref[...])
    blocks = entry_blocks(tile_ref)
    lanes = [tile_ref[b] & (LANES - 1) for b in blocks]
    keys = [tile_ref[b] >> 7 for b in blocks]
    tables = [
        surface[r : r + 1, c : c + LANES] for r in range(lines) for c in range(0, span, LANES)
    ]
    for (r, c), v in zip(blocks, picked(tables, keys, lanes)):
        part = c.start // LANES
        payload_ref[pl.ds(4 * r.start + part, SUBLANES, stride=4), :] = pieces_ref[r, c]
        payload_ref[pl.ds(4 * r.start + 2 + part, SUBLANES, stride=4), :] = v


def entry_sum(index_row, value_row, groups, order):
    entries = index_row.shape[1]
    group = order(index_row)
    hit = lax.broadcasted_iota(i32, (groups, entries), 0) == group
    high = value_row.astype(bf16).astype(f32)
    low = value_row - high
    weighted = jnp.concatenate(
        [jnp.where(hit, high, 0.0).astype(bf16), jnp.where(hit, low, 0.0).astype(bf16)], axis=0
    )
    lane = index_row & (LANES - 1)
    lane_hit = lax.broadcasted_iota(i32, (LANES, entries), 0) == lane
    return dot_nt(weighted, jnp.where(lane_hit, 1.0, 0.0).astype(bf16))


def joined_rows(ref, at):
    return jnp.concatenate([ref[at : at + 1, :], ref[at + 1 : at + 2, :]], axis=1)


def add_flux(received_ref, tile_ref, out_ref):
    entry_rows, slots = tile_ref.shape
    lines, span = out_ref.shape
    chunks = span // LANES
    groups = lines * chunks
    total = jnp.zeros((2 * groups, LANES), f32)
    for d in range(entry_rows):
        total = total + entry_sum(
            tile_ref[d : d + 1, :],
            joined_rows(received_ref, 4 * d),
            groups,
            lambda t: ((t >> 7) & (chunks - 1)) * lines + (t >> 10),
        )
    total = total[0:groups] + total[groups:]
    for c in range(chunks):
        out_ref[:, c * LANES : (c + 1) * LANES] = total[c * lines : (c + 1) * lines]


def add_warmth(received_ref, sender_ref, share_ref, flux_ref, other_flux_ref, out_ref, rate_ref):
    rate_ref[...] = flux_ref[...] + other_flux_ref[...]
    entry_rows, slots = sender_ref.shape
    groups = out_ref.shape[0]
    total = jnp.zeros((2 * groups, LANES), f32)
    for d in range(entry_rows):
        total = total + entry_sum(
            sender_ref[d : d + 1, :],
            joined_rows(received_ref, 4 * d + 2) * share_ref[d : d + 1, :],
            groups,
            lambda t: t >> 7,
        )
    out_ref[...] = total[0:groups] + total[groups:]


def on_device(
    air_profile_vector,
    profile_pass_kind,
    position_profile_map,
    sunlight_aerosol_drive,
    profile_link_operator,
    bottom_warmth_seen,
    intersect_sender_index,
    intersect_share,
    intersect_receiver_tile,
    marine_warmth_departure,
    earlier_bottom_inflow,
    marine_tile_indicator,
):
    rows, count = air_profile_vector.shape
    half = count // 2
    tiers, lines, span = marine_warmth_departure.shape
    entry_rows, slots = intersect_sender_index.shape
    n_dom = lax.axis_size("dom")
    n_block = lax.axis_size("comp") * n_dom
    place = position_profile_map.reshape(1, count)

    def shape(*dims):
        return jax.ShapeDtypeStruct(dims, f32)

    packed, mate, follow, level = call(
        pack_first,
        [
            shape(rows + SUBLANES, half),
            shape(STEPS + 3, 4, span),
            shape(STEPS + 3, 4, span),
            shape(STEPS, lines, span),
        ],
        [pl.BlockSpec(memory_space=pl.ANY)] * 5,
        (
            sunlight_aerosol_drive,
            place,
            marine_warmth_departure,
            earlier_bottom_inflow,
            marine_tile_indicator,
        ),
        "pack_first",
        1.5,
        scratch=[
            pltpu.VMEM((1, count), i32),
            pltpu.VMEM((STEPS + 1, lines, span), f32),
            pltpu.VMEM((lines, span), f32),
            pltpu.VMEM((lines, span), i32),
            pltpu.VMEM((SUBLANES, half), f32),
            pltpu.SemaphoreType.DMA((7,)),
        ],
        mib=56,
        out_specs=[
            pl.BlockSpec(memory_space=pl.ANY),
            whole(),
            whole(),
            pl.BlockSpec(memory_space=pl.ANY),
        ],
    )
    block_axes = ("comp", "dom")
    mates = [(i, i ^ 1) for i in range(n_block)]
    nexts = [(i, i + 1) for i in range(1, n_block - 1, 2)]
    nexts = nexts + [(j, i) for i, j in nexts]
    other = [(0, 1), (1, 0)]

    far = lax.ppermute(packed, "dom", [(i, (i + n_dom // 2) % n_dom) for i in range(n_dom)])
    level = lax.ppermute(level, "lev", other)
    mate = lax.ppermute(mate, block_axes, mates)
    follow = lax.ppermute(follow, block_axes, nexts)
    air_profile_updated, pieces = call(
        columns,
        [shape(rows, count), shape(entry_rows, slots)],
        [whole()] * 3 + [pl.BlockSpec((rows, half), lambda i: (0, 0))] + [whole()] * 5,
        (
            air_profile_vector,
            profile_pass_kind.reshape(1, count),
            place,
            sunlight_aerosol_drive,
            far,
            profile_link_operator,
            bottom_warmth_seen.reshape(1, count),
            intersect_sender_index,
            intersect_share,
        ),
        "columns",
        4.0,
        grid=(1,),
    )
    mate, follow, pieces = lax.optimization_barrier((mate, follow, pieces))
    part = pl.BlockSpec((STEPS + 3, 4, span), lambda i: (0, 0, 0))
    top = call(
        top_level,
        shape(lines, span),
        [pl.BlockSpec((STEPS + 1, lines, span), lambda i: (0, 0, 0)), part, part, whole(), whole()],
        (marine_warmth_departure, mate, follow, earlier_bottom_inflow, marine_tile_indicator),
        "top_level",
        1.0,
        grid=(1,),
    )
    top_far = lax.ppermute(top, "lev", [(0, 1)])

    later_level, top = lax.optimization_barrier((level, top))
    bulk = tiers - 1
    mate_bulk, follow_bulk = call(
        pack_bulk,
        [shape(bulk, 4, span), shape(bulk, 4, span)],
        [whole()] * 2,
        (marine_warmth_departure, later_level),
        "pack_bulk",
        1.0,
    )
    mate_bulk = lax.ppermute(mate_bulk, block_axes, mates)
    follow_bulk = lax.ppermute(follow_bulk, block_axes, nexts)

    payload = call(
        targets,
        shape(4 * entry_rows, LANES),
        [whole()] * 4,
        (intersect_receiver_tile, top, top_far, pieces),
        "targets",
        1.0,
    )
    received = lax.all_to_all(
        payload.reshape(entry_rows, 4, LANES), "dom", split_axis=0, concat_axis=0, tiled=True
    ).reshape(4 * entry_rows, LANES)

    partial_flux = call(
        add_flux,
        shape(lines, span),
        [whole()] * 2,
        (received, intersect_receiver_tile),
        "add_flux",
        20.0,
    )
    late_level, partial_flux = lax.optimization_barrier((level, partial_flux))
    theta = call(
        ocean,
        shape(tiers, lines, span),
        [whole()] * 8,
        (
            marine_warmth_departure,
            mate,
            follow,
            mate_bulk,
            follow_bulk,
            late_level,
            earlier_bottom_inflow,
            marine_tile_indicator,
        ),
        "ocean",
        6.0,
        scratch=[pltpu.VMEM((tiers + STEPS, 16, span), f32)] * 2 + [pltpu.VMEM((16, span), f32)] * 4,
    )

    other_flux = lax.ppermute(partial_flux, "lev", other)
    theta, other_flux = lax.optimization_barrier((theta, other_flux))
    air_bottom_warmth, marine_warming_rate = call(
        add_warmth,
        [shape(count // LANES, LANES), shape(lines, span)],
        [whole()] * 5,
        (received, intersect_sender_index, intersect_share, partial_flux, other_flux),
        "add_warmth",
        2.0,
    )
    air_bottom_warmth = air_bottom_warmth.reshape(count)
    return (air_profile_updated, theta, marine_warming_rate, air_bottom_warmth)


def solution(mesh):
    placed = (
        P(None, ("comp", "dom", "lev")),
        P(("comp", "dom", "lev")),
        P(("comp", "dom", "lev")),
        P(None, ("comp", "dom", "lev")),
        P(),
        P(("comp", "dom", "lev")),
        P(("comp", "dom", "lev"), None),
        P(("comp", "dom", "lev"), None),
        P(("comp", "dom", "lev"), None),
        P("lev", ("comp", "dom"), None),
        P(("comp", "dom"), None),
        P(("comp", "dom"), None),
    )
    return jax.shard_map(
        on_device,
        mesh=mesh,
        in_specs=placed,
        out_specs=(
            P(None, ("comp", "dom", "lev")),
            P("lev", ("comp", "dom"), None),
            P(("comp", "dom"), None),
            P(("comp", "dom", "lev")),
        ),
        check_vma=False,
    )
```

```python
import jax
import jax.numpy as jnp
from jax import lax
from jax.experimental import pallas as pl
from jax.experimental.pallas import tpu as pltpu
from jax.sharding import PartitionSpec as P

STEPS = 4
CLASSES = 3
LANES = 128
STREAM = 8
SUBLANES = 8

surface_exchange_factor = 0.8
humidity_exchange_factor = 0.5
tendency_scale = 0.5
horizontal_rate = 0.15
vertical_rate = 0.1
flux_gain = 0.5

f32 = jnp.float32
bf16 = jnp.bfloat16
i32 = jnp.int32


def whole():
    return pl.BlockSpec(memory_space=pltpu.VMEM)


def call(body, out_shapes, specs, args, name, microseconds, scratch=(), mib=32, grid=(), out_specs=None):
    one = not isinstance(out_shapes, (list, tuple))
    shapes = [out_shapes] if one else list(out_shapes)
    out = pl.pallas_call(
        body,
        out_shape=shapes,
        grid=grid,
        in_specs=specs,
        out_specs=out_specs or [whole() for _ in shapes],
        scratch_shapes=list(scratch),
        compiler_params=pltpu.CompilerParams(vmem_limit_bytes=mib * 1024 * 1024),
        cost_estimate=pl.CostEstimate(
            flops=int(microseconds * 1.0e9), bytes_accessed=int(microseconds * 3.0e6), transcendentals=0
        ),
        name=name,
    )(*args)
    return out[0] if one else out


def split(value):
    high = value.astype(bf16)
    low = (value - high.astype(f32)).astype(bf16)
    return high, low


def dot_nt(a, b):
    return lax.dot_general(a, b, (((1,), (1,)), ((), ())), preferred_element_type=f32)


def dot_nn(a, b):
    return lax.dot_general(a, b, (((1,), (0,)), ((), ())), preferred_element_type=f32)


def is_even():
    return lax.rem(lax.axis_index("dom"), 2) == 0


def edges(even, plane):
    low, high = plane[0:4, :], plane[4:8, :]
    return jnp.where(even, high, low), jnp.where(even, low, high)


def halo_rows(even, mate, other):
    return jnp.concatenate([jnp.where(even, mate, other), jnp.where(even, other, mate)], axis=0)


def pack_first(
    drive_ref,
    place_ref,
    theta_ref,
    inflow_ref,
    wet_ref,
    far_ref,
    mate_ref,
    next_ref,
    level_ref,
    place,
    surface,
    inflow,
    wet,
    sems,
):
    rows = drive_ref.shape[0]
    half = far_ref.shape[1]
    tiers = theta_ref.shape[0]
    base = jnp.where(lax.axis_index("lev") == 0, tiers - STEPS, 0)
    pairs = (
        (drive_ref.at[:, half : 2 * half], far_ref.at[0:rows, :]),
        (place_ref, place),
        (theta_ref.at[0 : STEPS + 1], surface),
        (inflow_ref, inflow),
        (wet_ref, wet),
        (theta_ref.at[pl.ds(base, STEPS)], level_ref),
    )
    copies = [pltpu.make_async_copy(a, b, sems.at[k]) for k, (a, b) in enumerate(pairs)]
    for copy in copies:
        copy.start()
    for copy in copies[1:5]:
        copy.wait()
    far = place[:, half : 2 * half].astype(f32)
    far_ref[rows : rows + SUBLANES, :] = jnp.broadcast_to(far, (SUBLANES, half))
    even = is_even()
    mate_ref[0], next_ref[0] = edges(even, inflow[...])
    mate_ref[1], next_ref[1] = edges(even, wet[...].astype(f32))
    for k in range(STEPS + 1):
        mate_ref[k + 2], next_ref[k + 2] = edges(even, surface[k])
    copies[0].wait()
    copies[5].wait()


def pack_bulk(theta_ref, level_ref, mate_ref, next_ref):
    even = is_even()
    skip = STEPS + 1
    deep = theta_ref.shape[0] - skip
    for k in range(deep):
        mate_ref[k], next_ref[k] = edges(even, theta_ref[k + skip])
    for j in range(STEPS):
        mate_ref[deep + j], next_ref[deep + j] = edges(even, level_ref[j])


def across(own, halo):
    span = own.shape[1]
    row = lax.broadcasted_iota(i32, own.shape, 0)
    first, last = row == 0, row == SUBLANES - 1
    own_less, halo_less = pltpu.roll(own, 1, 0), pltpu.roll(halo, 1, 0)
    own_more, halo_more = pltpu.roll(own, SUBLANES - 1, 0), pltpu.roll(halo, SUBLANES - 1, 0)
    own_sum = jnp.where(first, halo_less, own_less) + jnp.where(last, halo_more, own_more)
    own_sum = own_sum + (pltpu.roll(own, 1, 1) + pltpu.roll(own, span - 1, 1))
    halo_sum = jnp.where(first, own_less, halo_less) + jnp.where(last, own_more, halo_more)
    halo_sum = halo_sum + (pltpu.roll(halo, 1, 1) + pltpu.roll(halo, span - 1, 1))
    return own_sum, halo_sum


def top_level(theta_ref, mate_ref, next_ref, inflow_ref, wet_ref, out_ref):
    count = STEPS + 1
    even = is_even()

    def joined(k):
        return halo_rows(even, mate_ref[k], next_ref[k])

    wet = (wet_ref[...].astype(f32), joined(1))
    source = tuple(flux_gain * w * s for w, s in zip(wet, (inflow_ref[...], joined(0))))
    keep = tuple(1.0 - (4 * horizontal_rate + 2 * vertical_rate) * w for w in wet)
    side = tuple(horizontal_rate * w for w in wet)
    rise = tuple(vertical_rate * w for w in wet)
    levels = [(theta_ref[k], joined(k + 2)) for k in range(count)]
    for step in range(1, STEPS + 1):
        fresh = []
        for k in range(count - step):
            sums = across(*levels[k])
            value = []
            for part in range(2):
                vertical = levels[k + 1][part]
                if k > 0:
                    vertical = vertical + levels[k - 1][part]
                new = keep[part] * levels[k][part] + side[part] * sums[part] + rise[part] * vertical
                if k == 0:
                    new = new + source[part]
                value.append(new)
            fresh.append(tuple(value))
        levels = fresh
    out_ref[...] = levels[0][0]


def ocean(
    theta_ref,
    mate_ref,
    next_ref,
    mate_bulk_ref,
    next_bulk_ref,
    level_ref,
    inflow_ref,
    wet_ref,
    out_ref,
    even,
    odd,
    keep,
    side,
    rise,
    source,
    sems,
):
    tiers, lines, span = theta_ref.shape
    chunks = span // LANES
    places = tiers + STEPS
    skip = STEPS + 1
    lev = lax.axis_index("lev")
    lower = lev.astype(f32)
    upper = 1.0 - lower

    wet_own = wet_ref[...].astype(f32)
    even_block = is_even()
    wet_halo = halo_rows(even_block, mate_ref[1], next_ref[1])
    flow_halo = halo_rows(even_block, mate_ref[0], next_ref[0])
    for at, wet, flow in ((0, wet_own, inflow_ref[...]), (8, wet_halo, flow_halo)):
        rows = slice(at, at + 8)
        keep[rows, :] = 1.0 - (4 * horizontal_rate + 2 * vertical_rate) * wet
        side[rows, :] = horizontal_rate * wet
        rise[rows, :] = vertical_rate * wet
        source[rows, :] = (flux_gain * upper) * (wet * flow)

    for at in range(places):
        even[at, 0:8, :] = theta_ref[at] if at < tiers else level_ref[at - tiers]
        if at < skip:
            mate, other = mate_ref[at + 2], next_ref[at + 2]
        else:
            mate, other = mate_bulk_ref[at - skip], next_bulk_ref[at - skip]
        even[at, 8:12, :] = jnp.where(even_block, mate, other)
        even[at, 12:16, :] = jnp.where(even_block, other, mate)

    row = lax.broadcasted_iota(i32, (SUBLANES, LANES), 0)
    lane = lax.broadcasted_iota(i32, (SUBLANES, LANES), 1)
    first, last = row == 0, row == SUBLANES - 1
    lane_first, lane_last = lane == 0, lane == LANES - 1

    copies = []
    for step in range(1, STEPS + 1):
        held, fresh = (even, odd) if step % 2 else (odd, even)
        final = step == STEPS
        parts = (0,) if final else (0, 8)

        def advance(at, less, more, less_scale=None, more_scale=None, add_source=False):
            value = {
                (p, c): held[at, p : p + 8, c * LANES : (c + 1) * LANES]
                for p in (0, 8)
                for c in range(chunks)
            }
            right = {(p, c): pltpu.roll(value[p, c], 1, 1) for p in parts for c in range(chunks)}
            left = {(p, c): pltpu.roll(value[p, c], LANES - 1, 1) for p in parts for c in range(chunks)}
            for c in range(chunks):
                cols = slice(c * LANES, (c + 1) * LANES)
                own, halo = value[0, c], value[8, c]
                less_rows = {0: pltpu.roll(own, 1, 0), 8: pltpu.roll(halo, 1, 0)}
                more_rows = {0: pltpu.roll(own, 7, 0), 8: pltpu.roll(halo, 7, 0)}
                for p in parts:
                    around = jnp.where(first, less_rows[8 - p], less_rows[p])
                    around = around + jnp.where(last, more_rows[8 - p], more_rows[p])
                    along = jnp.where(lane_first, right[p, (c - 1) % chunks], right[p, c])
                    along = along + jnp.where(lane_last, left[p, (c + 1) % chunks], left[p, c])
                    rows = slice(p, p + 8)
                    a, b = held[less, rows, cols], held[more, rows, cols]
                    if less_scale is not None:
                        a = a * less_scale
                    if more_scale is not None:
                        b = b * more_scale
                    new = (
                        keep[rows, cols] * value[p, c]
                        + side[rows, cols] * (around + along)
                        + rise[rows, cols] * (a + b)
                    )
                    if add_source:
                        new = new + source[rows, cols]
                    fresh[at, rows, cols] = new

        advance(0, places - 1, 1, less_scale=lower, add_source=True)
        for at in range(1, tiers):
            advance(at, at - 1, at + 1, more_scale=upper if at == tiers - 1 else None)
            if final and (at + 1) % STREAM == 0:
                k = at // STREAM
                some = slice(k * STREAM, (k + 1) * STREAM)
                copies.append(
                    pltpu.make_async_copy(fresh.at[some, 0:8, :], out_ref.at[some], sems.at[k])
                )
                copies[-1].start()
        for j in range(STEPS - step):
            at = tiers + j + lev * step
            more = jnp.where(at == places - 1, 0, at + 1)
            advance(at, at - 1, more)
    for copy in copies:
        copy.wait()


def entry_blocks(ref):
    rows, slots = ref.shape
    return [
        (slice(r, r + SUBLANES), slice(c, c + LANES))
        for r in range(0, rows, SUBLANES)
        for c in range(0, slots, LANES)
    ]


def picked(tables, keys, lanes):
    found = [jnp.zeros((SUBLANES, LANES), f32) for _ in keys]
    for r, table in enumerate(tables):
        spread = jnp.broadcast_to(table, (SUBLANES, LANES))
        found = [
            jnp.where(
                k == r, jnp.take_along_axis(spread, l, axis=1, mode="promise_in_bounds"), v
            )
            for k, l, v in zip(keys, lanes, found)
        ]
    return found


def columns(
    state_ref,
    classes_ref,
    place_ref,
    drive_ref,
    far_ref,
    link_ref,
    warmth_ref,
    sender_ref,
    share_ref,
    out_ref,
    pieces_ref,
):
    rows, count = state_ref.shape
    half = drive_ref.shape[1]
    levels = rows // 2
    width = 256

    own_drive = jnp.concatenate(split(drive_ref[...]), axis=0)
    far_drive = jnp.concatenate(split(far_ref[0:rows, :]), axis=0)
    own_place = place_ref[:, 0:half]
    far_place = far_ref[rows : rows + 1, :].astype(i32)
    link_high, link_low = split(link_ref[...])
    link_both = jnp.concatenate([link_high, link_low], axis=0)

    flux = []
    for start in range(0, count, width):
        cols = slice(start, start + width)
        target = start + lax.broadcasted_iota(i32, (width, half), 0)
        own_pick = jnp.where(target == own_place, 1.0, 0.0).astype(bf16)
        far_pick = jnp.where(target == far_place, 1.0, 0.0).astype(bf16)
        both = dot_nt(own_drive, own_pick) + dot_nt(far_drive, far_pick)
        forcing = both[0:rows] + both[rows : 2 * rows]
        x = state_ref[:, cols]
        kinds = classes_ref[:, cols]
        for k in range(CLASSES):
            high, low = split(x)
            product = dot_nn(link_both, high)
            drive = product[0:rows] + (product[rows : 2 * rows] + dot_nn(link_high, low)) + forcing
            x = x + jnp.where(kinds > k, tendency_scale * jnp.tanh(drive), 0.0)
        out_ref[:, cols] = x
        flux.append(
            surface_exchange_factor * (x[levels - 1 : levels, :] - warmth_ref[:, cols])
            + humidity_exchange_factor * x[rows - 1 : rows, :]
        )
    flux = jnp.concatenate(flux, axis=1)

    blocks = entry_blocks(sender_ref)
    lanes = [sender_ref[b] & (LANES - 1) for b in blocks]
    keys = [sender_ref[b] >> 7 for b in blocks]
    tables = [flux[:, r * LANES : (r + 1) * LANES] for r in range(count // LANES)]
    for b, v in zip(blocks, picked(tables, keys, lanes)):
        pieces_ref[b] = share_ref[b] * v


def targets(tile_ref, top_ref, top_far_ref, pieces_ref, payload_ref):
    lines, span = top_ref.shape
    surface = jnp.where(lax.axis_index("lev") == 0, top_ref[...], top_far_ref[...])
    blocks = entry_blocks(tile_ref)
    lanes = [tile_ref[b] & (LANES - 1) for b in blocks]
    keys = [tile_ref[b] >> 7 for b in blocks]
    tables = [
        surface[r : r + 1, c : c + LANES] for r in range(lines) for c in range(0, span, LANES)
    ]
    for (r, c), v in zip(blocks, picked(tables, keys, lanes)):
        part = c.start // LANES
        payload_ref[pl.ds(4 * r.start + part, SUBLANES, stride=4), :] = pieces_ref[r, c]
        payload_ref[pl.ds(4 * r.start + 2 + part, SUBLANES, stride=4), :] = v


def entry_sum(index_row, value_row, groups, order):
    entries = index_row.shape[1]
    group = order(index_row)
    hit = lax.broadcasted_iota(i32, (groups, entries), 0) == group
    high = value_row.astype(bf16).astype(f32)
    low = value_row - high
    weighted = jnp.concatenate(
        [jnp.where(hit, high, 0.0).astype(bf16), jnp.where(hit, low, 0.0).astype(bf16)], axis=0
    )
    lane = index_row & (LANES - 1)
    lane_hit = lax.broadcasted_iota(i32, (LANES, entries), 0) == lane
    return dot_nt(weighted, jnp.where(lane_hit, 1.0, 0.0).astype(bf16))


def joined_rows(ref, at):
    return jnp.concatenate([ref[at : at + 1, :], ref[at + 1 : at + 2, :]], axis=1)


def add_flux(received_ref, tile_ref, out_ref):
    entry_rows, slots = tile_ref.shape
    lines, span = out_ref.shape
    chunks = span // LANES
    groups = lines * chunks
    total = jnp.zeros((2 * groups, LANES), f32)
    for d in range(entry_rows):
        total = total + entry_sum(
            tile_ref[d : d + 1, :],
            joined_rows(received_ref, 4 * d),
            groups,
            lambda t: ((t >> 7) & (chunks - 1)) * lines + (t >> 10),
        )
    total = total[0:groups] + total[groups:]
    for c in range(chunks):
        out_ref[:, c * LANES : (c + 1) * LANES] = total[c * lines : (c + 1) * lines]


def add_warmth(received_ref, sender_ref, share_ref, flux_ref, other_flux_ref, out_ref, rate_ref):
    rate_ref[...] = flux_ref[...] + other_flux_ref[...]
    entry_rows, slots = sender_ref.shape
    groups = out_ref.shape[0]
    total = jnp.zeros((2 * groups, LANES), f32)
    for d in range(entry_rows):
        total = total + entry_sum(
            sender_ref[d : d + 1, :],
            joined_rows(received_ref, 4 * d + 2) * share_ref[d : d + 1, :],
            groups,
            lambda t: t >> 7,
        )
    out_ref[...] = total[0:groups] + total[groups:]


def on_device(
    air_profile_vector,
    profile_pass_kind,
    position_profile_map,
    sunlight_aerosol_drive,
    profile_link_operator,
    bottom_warmth_seen,
    intersect_sender_index,
    intersect_share,
    intersect_receiver_tile,
    marine_warmth_departure,
    earlier_bottom_inflow,
    marine_tile_indicator,
):
    rows, count = air_profile_vector.shape
    half = count // 2
    tiers, lines, span = marine_warmth_departure.shape
    entry_rows, slots = intersect_sender_index.shape
    n_dom = lax.axis_size("dom")
    n_block = lax.axis_size("comp") * n_dom
    place = position_profile_map.reshape(1, count)

    def shape(*dims):
        return jax.ShapeDtypeStruct(dims, f32)

    packed, mate, follow, level = call(
        pack_first,
        [
            shape(rows + SUBLANES, half),
            shape(STEPS + 3, 4, span),
            shape(STEPS + 3, 4, span),
            shape(STEPS, lines, span),
        ],
        [pl.BlockSpec(memory_space=pl.ANY)] * 5,
        (
            sunlight_aerosol_drive,
            place,
            marine_warmth_departure,
            earlier_bottom_inflow,
            marine_tile_indicator,
        ),
        "pack_first",
        1.5,
        scratch=[
            pltpu.VMEM((1, count), i32),
            pltpu.VMEM((STEPS + 1, lines, span), f32),
            pltpu.VMEM((lines, span), f32),
            pltpu.VMEM((lines, span), i32),
            pltpu.SemaphoreType.DMA((6,)),
        ],
        mib=56,
    )
    block_axes = ("comp", "dom")
    mates = [(i, i ^ 1) for i in range(n_block)]
    nexts = [(i, i + 1) for i in range(1, n_block - 1, 2)]
    nexts = nexts + [(j, i) for i, j in nexts]
    other = [(0, 1), (1, 0)]

    far = lax.ppermute(packed, "dom", [(i, (i + n_dom // 2) % n_dom) for i in range(n_dom)])
    level = lax.ppermute(level, "lev", other)
    mate = lax.ppermute(mate, block_axes, mates)
    follow = lax.ppermute(follow, block_axes, nexts)
    air_profile_updated, pieces = call(
        columns,
        [shape(rows, count), shape(entry_rows, slots)],
        [whole()] * 3 + [pl.BlockSpec((rows, half), lambda i: (0, 0))] + [whole()] * 5,
        (
            air_profile_vector,
            profile_pass_kind.reshape(1, count),
            place,
            sunlight_aerosol_drive,
            far,
            profile_link_operator,
            bottom_warmth_seen.reshape(1, count),
            intersect_sender_index,
            intersect_share,
        ),
        "columns",
        4.0,
        grid=(1,),
    )
    mate, follow, pieces = lax.optimization_barrier((mate, follow, pieces))
    part = pl.BlockSpec((STEPS + 3, 4, span), lambda i: (0, 0, 0))
    top = call(
        top_level,
        shape(lines, span),
        [pl.BlockSpec((STEPS + 1, lines, span), lambda i: (0, 0, 0)), part, part, whole(), whole()],
        (marine_warmth_departure, mate, follow, earlier_bottom_inflow, marine_tile_indicator),
        "top_level",
        1.0,
        grid=(1,),
    )
    top_far = lax.ppermute(top, "lev", [(0, 1)])

    later_level, top = lax.optimization_barrier((level, top))
    bulk = tiers - 1
    mate_bulk, follow_bulk = call(
        pack_bulk,
        [shape(bulk, 4, span), shape(bulk, 4, span)],
        [whole()] * 2,
        (marine_warmth_departure, later_level),
        "pack_bulk",
        1.0,
    )
    mate_bulk = lax.ppermute(mate_bulk, block_axes, mates)
    follow_bulk = lax.ppermute(follow_bulk, block_axes, nexts)

    payload = call(
        targets,
        shape(4 * entry_rows, LANES),
        [whole()] * 4,
        (intersect_receiver_tile, top, top_far, pieces),
        "targets",
        8.0,
    )
    received = lax.all_to_all(
        payload.reshape(entry_rows, 4, LANES), "dom", split_axis=0, concat_axis=0, tiled=True
    ).reshape(4 * entry_rows, LANES)

    partial_flux = call(
        add_flux,
        shape(lines, span),
        [whole()] * 2,
        (received, intersect_receiver_tile),
        "add_flux",
        2.0,
    )
    late_level, partial_flux = lax.optimization_barrier((level, partial_flux))
    theta = call(
        ocean,
        shape(tiers, lines, span),
        [whole()] * 8,
        (
            marine_warmth_departure,
            mate,
            follow,
            mate_bulk,
            follow_bulk,
            late_level,
            earlier_bottom_inflow,
            marine_tile_indicator,
        ),
        "ocean",
        6.0,
        scratch=[pltpu.VMEM((tiers + STEPS, 16, span), f32)] * 2 + [pltpu.VMEM((16, span), f32)] * 4
        + [pltpu.SemaphoreType.DMA((tiers // STREAM,))],
        out_specs=[pl.BlockSpec(memory_space=pl.ANY)],
    )

    other_flux = lax.ppermute(partial_flux, "lev", other)
    theta, other_flux = lax.optimization_barrier((theta, other_flux))
    air_bottom_warmth, marine_warming_rate = call(
        add_warmth,
        [shape(count // LANES, LANES), shape(lines, span)],
        [whole()] * 5,
        (received, intersect_sender_index, intersect_share, partial_flux, other_flux),
        "add_warmth",
        2.0,
    )
    air_bottom_warmth = air_bottom_warmth.reshape(count)
    return (air_profile_updated, theta, marine_warming_rate, air_bottom_warmth)


def solution(mesh):
    placed = (
        P(None, ("comp", "dom", "lev")),
        P(("comp", "dom", "lev")),
        P(("comp", "dom", "lev")),
        P(None, ("comp", "dom", "lev")),
        P(),
        P(("comp", "dom", "lev")),
        P(("comp", "dom", "lev"), None),
        P(("comp", "dom", "lev"), None),
        P(("comp", "dom", "lev"), None),
        P("lev", ("comp", "dom"), None),
        P(("comp", "dom"), None),
        P(("comp", "dom"), None),
    )
    return jax.shard_map(
        on_device,
        mesh=mesh,
        in_specs=placed,
        out_specs=(
            P(None, ("comp", "dom", "lev")),
            P("lev", ("comp", "dom"), None),
            P(("comp", "dom"), None),
            P(("comp", "dom", "lev")),
        ),
        check_vma=False,
    )
```

```python
import jax
import jax.numpy as jnp
from jax import lax
from jax.experimental import pallas as pl
from jax.experimental.pallas import tpu as pltpu
from jax.sharding import PartitionSpec as P

STEPS = 4
CLASSES = 3
LANES = 128
STREAM = 8
SUBLANES = 8

surface_exchange_factor = 0.8
humidity_exchange_factor = 0.5
tendency_scale = 0.5
horizontal_rate = 0.15
vertical_rate = 0.1
flux_gain = 0.5

f32 = jnp.float32
bf16 = jnp.bfloat16
i32 = jnp.int32


def whole():
    return pl.BlockSpec(memory_space=pltpu.VMEM)


def call(body, out_shapes, specs, args, name, microseconds, scratch=(), mib=32, grid=(), out_specs=None):
    one = not isinstance(out_shapes, (list, tuple))
    shapes = [out_shapes] if one else list(out_shapes)
    out = pl.pallas_call(
        body,
        out_shape=shapes,
        grid=grid,
        in_specs=specs,
        out_specs=out_specs or [whole() for _ in shapes],
        scratch_shapes=list(scratch),
        compiler_params=pltpu.CompilerParams(vmem_limit_bytes=mib * 1024 * 1024),
        cost_estimate=pl.CostEstimate(
            flops=int(microseconds * 1.0e9), bytes_accessed=int(microseconds * 3.0e6), transcendentals=0
        ),
        name=name,
    )(*args)
    return out[0] if one else out


def split(value):
    high = value.astype(bf16)
    low = (value - high.astype(f32)).astype(bf16)
    return high, low


def dot_nt(a, b):
    return lax.dot_general(a, b, (((1,), (1,)), ((), ())), preferred_element_type=f32)


def dot_nn(a, b):
    return lax.dot_general(a, b, (((1,), (0,)), ((), ())), preferred_element_type=f32)


def is_even():
    return lax.rem(lax.axis_index("dom"), 2) == 0


def edges(even, plane):
    low, high = plane[0:4, :], plane[4:8, :]
    return jnp.where(even, high, low), jnp.where(even, low, high)


def halo_rows(even, mate, other):
    return jnp.concatenate([jnp.where(even, mate, other), jnp.where(even, other, mate)], axis=0)


def pack_first(
    drive_ref,
    place_ref,
    theta_ref,
    inflow_ref,
    wet_ref,
    far_ref,
    mate_ref,
    next_ref,
    level_ref,
    place,
    surface,
    inflow,
    wet,
    sems,
):
    rows = drive_ref.shape[0]
    half = far_ref.shape[1]
    tiers = theta_ref.shape[0]
    base = jnp.where(lax.axis_index("lev") == 0, tiers - STEPS, 0)
    pairs = (
        (drive_ref.at[:, half : 2 * half], far_ref.at[0:rows, :]),
        (place_ref, place),
        (theta_ref.at[0 : STEPS + 1], surface),
        (inflow_ref, inflow),
        (wet_ref, wet),
        (theta_ref.at[pl.ds(base, STEPS)], level_ref),
    )
    copies = [pltpu.make_async_copy(a, b, sems.at[k]) for k, (a, b) in enumerate(pairs)]
    for copy in copies:
        copy.start()
    for copy in copies[1:5]:
        copy.wait()
    far = place[:, half : 2 * half].astype(f32)
    far_ref[rows : rows + SUBLANES, :] = jnp.broadcast_to(far, (SUBLANES, half))
    even = is_even()
    mate_ref[0], next_ref[0] = edges(even, inflow[...])
    mate_ref[1], next_ref[1] = edges(even, wet[...].astype(f32))
    for k in range(STEPS + 1):
        mate_ref[k + 2], next_ref[k + 2] = edges(even, surface[k])
    copies[0].wait()
    copies[5].wait()


def pack_bulk(theta_ref, level_ref, mate_ref, next_ref):
    even = is_even()
    skip = STEPS + 1
    deep = theta_ref.shape[0] - skip
    for k in range(deep):
        mate_ref[k], next_ref[k] = edges(even, theta_ref[k + skip])
    for j in range(STEPS):
        mate_ref[deep + j], next_ref[deep + j] = edges(even, level_ref[j])


def across(own, halo):
    span = own.shape[1]
    row = lax.broadcasted_iota(i32, own.shape, 0)
    first, last = row == 0, row == SUBLANES - 1
    own_less, halo_less = pltpu.roll(own, 1, 0), pltpu.roll(halo, 1, 0)
    own_more, halo_more = pltpu.roll(own, SUBLANES - 1, 0), pltpu.roll(halo, SUBLANES - 1, 0)
    own_sum = jnp.where(first, halo_less, own_less) + jnp.where(last, halo_more, own_more)
    own_sum = own_sum + (pltpu.roll(own, 1, 1) + pltpu.roll(own, span - 1, 1))
    halo_sum = jnp.where(first, own_less, halo_less) + jnp.where(last, own_more, halo_more)
    halo_sum = halo_sum + (pltpu.roll(halo, 1, 1) + pltpu.roll(halo, span - 1, 1))
    return own_sum, halo_sum


def top_level(theta_ref, mate_ref, next_ref, inflow_ref, wet_ref, out_ref):
    count = STEPS + 1
    even = is_even()

    def joined(k):
        return halo_rows(even, mate_ref[k], next_ref[k])

    wet = (wet_ref[...].astype(f32), joined(1))
    source = tuple(flux_gain * w * s for w, s in zip(wet, (inflow_ref[...], joined(0))))
    keep = tuple(1.0 - (4 * horizontal_rate + 2 * vertical_rate) * w for w in wet)
    side = tuple(horizontal_rate * w for w in wet)
    rise = tuple(vertical_rate * w for w in wet)
    levels = [(theta_ref[k], joined(k + 2)) for k in range(count)]
    for step in range(1, STEPS + 1):
        fresh = []
        for k in range(count - step):
            sums = across(*levels[k])
            value = []
            for part in range(2):
                vertical = levels[k + 1][part]
                if k > 0:
                    vertical = vertical + levels[k - 1][part]
                new = keep[part] * levels[k][part] + side[part] * sums[part] + rise[part] * vertical
                if k == 0:
                    new = new + source[part]
                value.append(new)
            fresh.append(tuple(value))
        levels = fresh
    out_ref[...] = levels[0][0]


def ocean(
    theta_ref,
    mate_ref,
    next_ref,
    mate_bulk_ref,
    next_bulk_ref,
    level_ref,
    inflow_ref,
    wet_ref,
    out_ref,
    even,
    odd,
    keep,
    side,
    rise,
    source,
    sems,
):
    tiers, lines, span = theta_ref.shape
    chunks = span // LANES
    places = tiers + STEPS
    skip = STEPS + 1
    lev = lax.axis_index("lev")
    lower = lev.astype(f32)
    upper = 1.0 - lower

    wet_own = wet_ref[...].astype(f32)
    even_block = is_even()
    wet_halo = halo_rows(even_block, mate_ref[1], next_ref[1])
    flow_halo = halo_rows(even_block, mate_ref[0], next_ref[0])
    for at, wet, flow in ((0, wet_own, inflow_ref[...]), (8, wet_halo, flow_halo)):
        rows = slice(at, at + 8)
        keep[rows, :] = 1.0 - (4 * horizontal_rate + 2 * vertical_rate) * wet
        side[rows, :] = horizontal_rate * wet
        rise[rows, :] = vertical_rate * wet
        source[rows, :] = (flux_gain * upper) * (wet * flow)

    for at in range(places):
        if at >= tiers:
            even[at, 0:8, :] = level_ref[at - tiers]
        elif at in (0, tiers - 1):
            even[at, 0:8, :] = theta_ref[at]
        if at < skip:
            mate, other = mate_ref[at + 2], next_ref[at + 2]
        else:
            mate, other = mate_bulk_ref[at - skip], next_bulk_ref[at - skip]
        even[at, 8:12, :] = jnp.where(even_block, mate, other)
        even[at, 12:16, :] = jnp.where(even_block, other, mate)

    row = lax.broadcasted_iota(i32, (SUBLANES, LANES), 0)
    lane = lax.broadcasted_iota(i32, (SUBLANES, LANES), 1)
    first, last = row == 0, row == SUBLANES - 1
    lane_first, lane_last = lane == 0, lane == LANES - 1

    copies = []
    for step in range(1, STEPS + 1):
        held, fresh = (even, odd) if step % 2 else (odd, even)
        final = step == STEPS
        parts = (0,) if final else (0, 8)

        def advance(at, less, more, less_scale=None, more_scale=None, add_source=False):
            def plane(index, p, cols):
                if step == 1 and p == 0 and isinstance(index, int) and index < tiers:
                    return theta_ref[index, :, cols]
                return held[index, p : p + 8, cols]

            value = {
                (p, c): plane(at, p, slice(c * LANES, (c + 1) * LANES))
                for p in (0, 8)
                for c in range(chunks)
            }
            right = {(p, c): pltpu.roll(value[p, c], 1, 1) for p in parts for c in range(chunks)}
            left = {(p, c): pltpu.roll(value[p, c], LANES - 1, 1) for p in parts for c in range(chunks)}
            for c in range(chunks):
                cols = slice(c * LANES, (c + 1) * LANES)
                for p in parts:
                    mine, next_to = value[p, c], value[8 - p, c]
                    around = pltpu.roll(jnp.where(last, next_to, mine), 1, 0)
                    around = around + pltpu.roll(jnp.where(first, next_to, mine), 7, 0)
                    along = jnp.where(lane_first, right[p, (c - 1) % chunks], right[p, c])
                    along = along + jnp.where(lane_last, left[p, (c + 1) % chunks], left[p, c])
                    rows = slice(p, p + 8)
                    a, b = plane(less, p, cols), plane(more, p, cols)
                    if less_scale is not None:
                        a = a * less_scale
                    if more_scale is not None:
                        b = b * more_scale
                    new = (
                        keep[rows, cols] * value[p, c]
                        + side[rows, cols] * (around + along)
                        + rise[rows, cols] * (a + b)
                    )
                    if add_source:
                        new = new + source[rows, cols]
                    fresh[at, rows, cols] = new

        advance(0, places - 1, 1, less_scale=lower, add_source=True)
        for at in range(1, tiers):
            advance(at, at - 1, at + 1, more_scale=upper if at == tiers - 1 else None)
            if final and (at + 1) % STREAM == 0:
                k = at // STREAM
                some = slice(k * STREAM, (k + 1) * STREAM)
                copies.append(
                    pltpu.make_async_copy(fresh.at[some, 0:8, :], out_ref.at[some], sems.at[k])
                )
                copies[-1].start()
        for j in range(STEPS - step):
            at = tiers + j + lev * step
            more = jnp.where(at == places - 1, 0, at + 1)
            advance(at, at - 1, more)
    for copy in copies:
        copy.wait()


def entry_blocks(ref):
    rows, slots = ref.shape
    return [
        (slice(r, r + SUBLANES), slice(c, c + LANES))
        for r in range(0, rows, SUBLANES)
        for c in range(0, slots, LANES)
    ]


def picked(tables, keys, lanes):
    found = [jnp.zeros((SUBLANES, LANES), f32) for _ in keys]
    for r, table in enumerate(tables):
        spread = jnp.broadcast_to(table, (SUBLANES, LANES))
        found = [
            jnp.where(
                k == r, jnp.take_along_axis(spread, l, axis=1, mode="promise_in_bounds"), v
            )
            for k, l, v in zip(keys, lanes, found)
        ]
    return found


def own_forcing(place_ref, drive_ref, out_ref):
    rows, half = drive_ref.shape
    count = out_ref.shape[1]
    drive = jnp.concatenate(split(drive_ref[...]), axis=0)
    place = place_ref[:, 0:half]
    width = 256
    for start in range(0, count, width):
        target = start + lax.broadcasted_iota(i32, (width, half), 0)
        both = dot_nt(drive, jnp.where(target == place, 1.0, 0.0).astype(bf16))
        out_ref[:, start : start + width] = both[0:rows] + both[rows : 2 * rows]


def columns(
    state_ref,
    classes_ref,
    forcing_ref,
    far_ref,
    link_ref,
    warmth_ref,
    sender_ref,
    share_ref,
    out_ref,
    pieces_ref,
    result,
    sems,
):
    rows, count = state_ref.shape
    half = far_ref.shape[1]
    levels = rows // 2
    width = 256

    far_drive = jnp.concatenate(split(far_ref[0:rows, :]), axis=0)
    far_place = far_ref[rows : rows + 1, :].astype(i32)
    link_high, link_low = split(link_ref[...])
    link_both = jnp.concatenate([link_high, link_low], axis=0)

    chunks = [slice(start, start + width) for start in range(0, count, width)]
    forcing = []
    for cols in chunks:
        target = cols.start + lax.broadcasted_iota(i32, (width, half), 0)
        far_pick = jnp.where(target == far_place, 1.0, 0.0).astype(bf16)
        both = dot_nt(far_drive, far_pick)
        forcing.append(forcing_ref[:, cols] + (both[0:rows] + both[rows : 2 * rows]))
    states = [state_ref[:, cols] for cols in chunks]
    for k in range(CLASSES):
        for c, cols in enumerate(chunks):
            x = states[c]
            high, low = split(x)
            product = dot_nn(link_both, high)
            drive = product[0:rows] + (product[rows : 2 * rows] + dot_nn(link_high, low)) + forcing[c]
            states[c] = x + jnp.where(classes_ref[:, cols] > k, tendency_scale * jnp.tanh(drive), 0.0)
    copies = []
    flux = []
    for c, cols in enumerate(chunks):
        x = states[c]
        result[:, cols] = x
        copies.append(pltpu.make_async_copy(result.at[:, cols], out_ref.at[:, cols], sems.at[c]))
        copies[c].start()
        flux.append(
            surface_exchange_factor * (x[levels - 1 : levels, :] - warmth_ref[:, cols])
            + humidity_exchange_factor * x[rows - 1 : rows, :]
        )
    flux = jnp.concatenate(flux, axis=1)

    blocks = entry_blocks(sender_ref)
    lanes = [sender_ref[b] & (LANES - 1) for b in blocks]
    keys = [sender_ref[b] >> 7 for b in blocks]
    tables = [flux[:, r * LANES : (r + 1) * LANES] for r in range(count // LANES)]
    for b, v in zip(blocks, picked(tables, keys, lanes)):
        pieces_ref[b] = share_ref[b] * v
    for copy in copies:
        copy.wait()


def targets(tile_ref, top_ref, top_far_ref, pieces_ref, payload_ref):
    lines, span = top_ref.shape
    surface = jnp.where(lax.axis_index("lev") == 0, top_ref[...], top_far_ref[...])
    blocks = entry_blocks(tile_ref)
    lanes = [tile_ref[b] & (LANES - 1) for b in blocks]
    keys = [tile_ref[b] >> 7 for b in blocks]
    tables = [
        surface[r : r + 1, c : c + LANES] for r in range(lines) for c in range(0, span, LANES)
    ]
    for (r, c), v in zip(blocks, picked(tables, keys, lanes)):
        part = c.start // LANES
        payload_ref[pl.ds(4 * r.start + part, SUBLANES, stride=4), :] = pieces_ref[r, c]
        payload_ref[pl.ds(4 * r.start + 2 + part, SUBLANES, stride=4), :] = v


def entry_sum(index_row, value_row, groups, order, width=LANES):
    entries = index_row.shape[1]
    group = order(index_row)
    hit = lax.broadcasted_iota(i32, (groups, entries), 0) == group
    high = value_row.astype(bf16).astype(f32)
    low = value_row - high
    weighted = jnp.concatenate(
        [jnp.where(hit, high, 0.0).astype(bf16), jnp.where(hit, low, 0.0).astype(bf16)], axis=0
    )
    lane = index_row & (width - 1)
    lane_hit = lax.broadcasted_iota(i32, (width, entries), 0) == lane
    return dot_nt(weighted, jnp.where(lane_hit, 1.0, 0.0).astype(bf16))


def joined_rows(ref, at):
    return jnp.concatenate([ref[at : at + 1, :], ref[at + 1 : at + 2, :]], axis=1)


def add_flux(received_ref, tile_ref, out_ref):
    entry_rows, slots = tile_ref.shape
    lines, span = out_ref.shape
    chunks = span // LANES
    groups = lines * chunks
    total = jnp.zeros((2 * groups, LANES), f32)
    for d in range(entry_rows):
        total = total + entry_sum(
            tile_ref[d : d + 1, :],
            joined_rows(received_ref, 4 * d),
            groups,
            lambda t: ((t >> 7) & (chunks - 1)) * lines + (t >> 10),
        )
    total = total[0:groups] + total[groups:]
    for c in range(chunks):
        out_ref[:, c * LANES : (c + 1) * LANES] = total[c * lines : (c + 1) * lines]


def add_warmth(received_ref, sender_ref, share_ref, flux_ref, other_flux_ref, out_ref, rate_ref):
    rate_ref[...] = flux_ref[...] + other_flux_ref[...]
    entry_rows, slots = sender_ref.shape
    lines = out_ref.shape[0]
    parts = 4
    width = LANES // parts
    groups = lines * parts
    total = jnp.zeros((2 * groups, width), f32)
    for d in range(entry_rows):
        total = total + entry_sum(
            sender_ref[d : d + 1, :],
            joined_rows(received_ref, 4 * d + 2) * share_ref[d : d + 1, :],
            groups,
            lambda t: ((t >> 5) & (parts - 1)) * lines + (t >> 7),
            width,
        )
    total = total[0:groups] + total[groups:]
    for k in range(parts):
        out_ref[:, k * width : (k + 1) * width] = total[k * lines : (k + 1) * lines]


def on_device(
    air_profile_vector,
    profile_pass_kind,
    position_profile_map,
    sunlight_aerosol_drive,
    profile_link_operator,
    bottom_warmth_seen,
    intersect_sender_index,
    intersect_share,
    intersect_receiver_tile,
    marine_warmth_departure,
    earlier_bottom_inflow,
    marine_tile_indicator,
):
    rows, count = air_profile_vector.shape
    half = count // 2
    tiers, lines, span = marine_warmth_departure.shape
    entry_rows, slots = intersect_sender_index.shape
    n_dom = lax.axis_size("dom")
    n_block = lax.axis_size("comp") * n_dom
    place = position_profile_map.reshape(1, count)

    def shape(*dims):
        return jax.ShapeDtypeStruct(dims, f32)

    packed, mate, follow, level = call(
        pack_first,
        [
            shape(rows + SUBLANES, half),
            shape(STEPS + 3, 4, span),
            shape(STEPS + 3, 4, span),
            shape(STEPS, lines, span),
        ],
        [pl.BlockSpec(memory_space=pl.ANY)] * 5,
        (
            sunlight_aerosol_drive,
            place,
            marine_warmth_departure,
            earlier_bottom_inflow,
            marine_tile_indicator,
        ),
        "pack_first",
        1.5,
        scratch=[
            pltpu.VMEM((1, count), i32),
            pltpu.VMEM((STEPS + 1, lines, span), f32),
            pltpu.VMEM((lines, span), f32),
            pltpu.VMEM((lines, span), i32),
            pltpu.SemaphoreType.DMA((6,)),
        ],
        mib=56,
    )
    block_axes = ("comp", "dom")
    mates = [(i, i ^ 1) for i in range(n_block)]
    nexts = [(i, i + 1) for i in range(1, n_block - 1, 2)]
    nexts = nexts + [(j, i) for i, j in nexts]
    other = [(0, 1), (1, 0)]

    far = lax.ppermute(packed, "dom", [(i, (i + n_dom // 2) % n_dom) for i in range(n_dom)])
    level = lax.ppermute(level, "lev", other)
    mate = lax.ppermute(mate, block_axes, mates)
    follow = lax.ppermute(follow, block_axes, nexts)
    forcing = call(
        own_forcing,
        shape(rows, count),
        [whole(), pl.BlockSpec((rows, half), lambda i: (0, 0))],
        (place, sunlight_aerosol_drive),
        "own_forcing",
        1.0,
        grid=(1,),
    )
    air_profile_updated, pieces = call(
        columns,
        [shape(rows, count), shape(entry_rows, slots)],
        [whole()] * 8,
        (
            air_profile_vector,
            profile_pass_kind.reshape(1, count),
            forcing,
            far,
            profile_link_operator,
            bottom_warmth_seen.reshape(1, count),
            intersect_sender_index,
            intersect_share,
        ),
        "columns",
        3.0,
        scratch=[pltpu.VMEM((rows, count), f32), pltpu.SemaphoreType.DMA((count // 256,))],
        out_specs=[pl.BlockSpec(memory_space=pl.ANY), whole()],
    )
    mate, follow, pieces = lax.optimization_barrier((mate, follow, pieces))
    part = pl.BlockSpec((STEPS + 3, 4, span), lambda i: (0, 0, 0))
    top = call(
        top_level,
        shape(lines, span),
        [pl.BlockSpec((STEPS + 1, lines, span), lambda i: (0, 0, 0)), part, part, whole(), whole()],
        (marine_warmth_departure, mate, follow, earlier_bottom_inflow, marine_tile_indicator),
        "top_level",
        1.0,
        grid=(1,),
    )
    top_far = lax.ppermute(top, "lev", [(0, 1)])

    later_level, top = lax.optimization_barrier((level, top))
    bulk = tiers - 1
    mate_bulk, follow_bulk = call(
        pack_bulk,
        [shape(bulk, 4, span), shape(bulk, 4, span)],
        [whole()] * 2,
        (marine_warmth_departure, later_level),
        "pack_bulk",
        1.0,
    )
    mate_bulk = lax.ppermute(mate_bulk, block_axes, mates)
    follow_bulk = lax.ppermute(follow_bulk, block_axes, nexts)

    payload = call(
        targets,
        shape(4 * entry_rows, LANES),
        [whole()] * 4,
        (intersect_receiver_tile, top, top_far, pieces),
        "targets",
        8.0,
    )
    received = lax.all_to_all(
        payload.reshape(entry_rows, 4, LANES), "dom", split_axis=0, concat_axis=0, tiled=True
    ).reshape(4 * entry_rows, LANES)

    partial_flux = call(
        add_flux,
        shape(lines, span),
        [whole()] * 2,
        (received, intersect_receiver_tile),
        "add_flux",
        2.0,
    )
    late_level, partial_flux = lax.optimization_barrier((level, partial_flux))
    theta = call(
        ocean,
        shape(tiers, lines, span),
        [whole()] * 8,
        (
            marine_warmth_departure,
            mate,
            follow,
            mate_bulk,
            follow_bulk,
            late_level,
            earlier_bottom_inflow,
            marine_tile_indicator,
        ),
        "ocean",
        6.0,
        scratch=[pltpu.VMEM((tiers + STEPS, 16, span), f32)] * 2 + [pltpu.VMEM((16, span), f32)] * 4
        + [pltpu.SemaphoreType.DMA((tiers // STREAM,))],
        out_specs=[pl.BlockSpec(memory_space=pl.ANY)],
    )

    other_flux = lax.ppermute(partial_flux, "lev", other)
    theta, other_flux = lax.optimization_barrier((theta, other_flux))
    air_bottom_warmth, marine_warming_rate = call(
        add_warmth,
        [shape(count // LANES, LANES), shape(lines, span)],
        [whole()] * 5,
        (received, intersect_sender_index, intersect_share, partial_flux, other_flux),
        "add_warmth",
        2.0,
    )
    air_bottom_warmth = air_bottom_warmth.reshape(count)
    return (air_profile_updated, theta, marine_warming_rate, air_bottom_warmth)


def solution(mesh):
    placed = (
        P(None, ("comp", "dom", "lev")),
        P(("comp", "dom", "lev")),
        P(("comp", "dom", "lev")),
        P(None, ("comp", "dom", "lev")),
        P(),
        P(("comp", "dom", "lev")),
        P(("comp", "dom", "lev"), None),
        P(("comp", "dom", "lev"), None),
        P(("comp", "dom", "lev"), None),
        P("lev", ("comp", "dom"), None),
        P(("comp", "dom"), None),
        P(("comp", "dom"), None),
    )
    return jax.shard_map(
        on_device,
        mesh=mesh,
        in_specs=placed,
        out_specs=(
            P(None, ("comp", "dom", "lev")),
            P("lev", ("comp", "dom"), None),
            P(("comp", "dom"), None),
            P(("comp", "dom", "lev")),
        ),
        check_vma=False,
    )
```

```python
import functools

import jax
import jax.numpy as jnp
from jax import lax
from jax.experimental import pallas as pl
from jax.experimental.pallas import tpu as pltpu
from jax.sharding import PartitionSpec as P

STEPS = 4
CLASSES = 3
LANES = 128
STREAM = 8
SUBLANES = 8

surface_exchange_factor = 0.8
humidity_exchange_factor = 0.5
tendency_scale = 0.5
horizontal_rate = 0.15
vertical_rate = 0.1
flux_gain = 0.5

f32 = jnp.float32
bf16 = jnp.bfloat16
i32 = jnp.int32


def whole():
    return pl.BlockSpec(memory_space=pltpu.VMEM)


def call(body, out_shapes, specs, args, name, microseconds, scratch=(), mib=32, grid=(), out_specs=None):
    one = not isinstance(out_shapes, (list, tuple))
    shapes = [out_shapes] if one else list(out_shapes)
    out = pl.pallas_call(
        body,
        out_shape=shapes,
        grid=grid,
        in_specs=specs,
        out_specs=out_specs or [whole() for _ in shapes],
        scratch_shapes=list(scratch),
        compiler_params=pltpu.CompilerParams(vmem_limit_bytes=mib * 1024 * 1024),
        cost_estimate=pl.CostEstimate(
            flops=int(microseconds * 1.0e9), bytes_accessed=int(microseconds * 3.0e6), transcendentals=0
        ),
        name=name,
    )(*args)
    return out[0] if one else out


def split(value):
    high = value.astype(bf16)
    low = (value - high.astype(f32)).astype(bf16)
    return high, low


def dot_nt(a, b):
    return lax.dot_general(a, b, (((1,), (1,)), ((), ())), preferred_element_type=f32)


def dot_nn(a, b):
    return lax.dot_general(a, b, (((1,), (0,)), ((), ())), preferred_element_type=f32)


def is_even():
    return lax.rem(lax.axis_index("dom"), 2) == 0


def edges(even, plane):
    low, high = plane[0:4, :], plane[4:8, :]
    return jnp.where(even, high, low), jnp.where(even, low, high)


def halo_rows(even, mate, other):
    return jnp.concatenate([jnp.where(even, mate, other), jnp.where(even, other, mate)], axis=0)


def pack_first(
    drive_ref,
    place_ref,
    theta_ref,
    inflow_ref,
    wet_ref,
    far_ref,
    mate_ref,
    next_ref,
    level_ref,
    place,
    surface,
    inflow,
    wet,
    sems,
):
    rows = drive_ref.shape[0]
    half = far_ref.shape[1]
    tiers = theta_ref.shape[0]
    base = jnp.where(lax.axis_index("lev") == 0, tiers - STEPS, 0)
    pairs = (
        (drive_ref.at[:, half : 2 * half], far_ref.at[0:rows, :]),
        (place_ref, place),
        (theta_ref.at[0 : STEPS + 1], surface),
        (inflow_ref, inflow),
        (wet_ref, wet),
        (theta_ref.at[pl.ds(base, STEPS)], level_ref),
    )
    copies = [pltpu.make_async_copy(a, b, sems.at[k]) for k, (a, b) in enumerate(pairs)]
    for copy in copies:
        copy.start()
    for copy in copies[1:5]:
        copy.wait()
    far = place[:, half : 2 * half].astype(f32)
    far_ref[rows : rows + SUBLANES, :] = jnp.broadcast_to(far, (SUBLANES, half))
    even = is_even()
    mate_ref[0], next_ref[0] = edges(even, inflow[...])
    mate_ref[1], next_ref[1] = edges(even, wet[...].astype(f32))
    for k in range(STEPS + 1):
        mate_ref[k + 2], next_ref[k + 2] = edges(even, surface[k])
    copies[0].wait()
    copies[5].wait()


def pack_bulk(side, theta_ref, level_ref, out_ref):
    even = is_even()
    skip = STEPS + 1
    deep = theta_ref.shape[0] - skip
    for k in range(deep):
        out_ref[k] = edges(even, theta_ref[k + skip])[side]
    for j in range(STEPS):
        out_ref[deep + j] = edges(even, level_ref[j])[side]


def across(own, halo):
    span = own.shape[1]
    row = lax.broadcasted_iota(i32, own.shape, 0)
    first, last = row == 0, row == SUBLANES - 1
    own_less, halo_less = pltpu.roll(own, 1, 0), pltpu.roll(halo, 1, 0)
    own_more, halo_more = pltpu.roll(own, SUBLANES - 1, 0), pltpu.roll(halo, SUBLANES - 1, 0)
    own_sum = jnp.where(first, halo_less, own_less) + jnp.where(last, halo_more, own_more)
    own_sum = own_sum + (pltpu.roll(own, 1, 1) + pltpu.roll(own, span - 1, 1))
    halo_sum = jnp.where(first, own_less, halo_less) + jnp.where(last, own_more, halo_more)
    halo_sum = halo_sum + (pltpu.roll(halo, 1, 1) + pltpu.roll(halo, span - 1, 1))
    return own_sum, halo_sum


def top_level(theta_ref, mate_ref, next_ref, inflow_ref, wet_ref, out_ref):
    count = STEPS + 1
    even = is_even()

    def joined(k):
        return halo_rows(even, mate_ref[k], next_ref[k])

    wet = (wet_ref[...].astype(f32), joined(1))
    source = tuple(flux_gain * w * s for w, s in zip(wet, (inflow_ref[...], joined(0))))
    keep = tuple(1.0 - (4 * horizontal_rate + 2 * vertical_rate) * w for w in wet)
    side = tuple(horizontal_rate * w for w in wet)
    rise = tuple(vertical_rate * w for w in wet)
    levels = [(theta_ref[k], joined(k + 2)) for k in range(count)]
    for step in range(1, STEPS + 1):
        fresh = []
        for k in range(count - step):
            sums = across(*levels[k])
            value = []
            for part in range(2):
                vertical = levels[k + 1][part]
                if k > 0:
                    vertical = vertical + levels[k - 1][part]
                new = keep[part] * levels[k][part] + side[part] * sums[part] + rise[part] * vertical
                if k == 0:
                    new = new + source[part]
                value.append(new)
            fresh.append(tuple(value))
        levels = fresh
    out_ref[...] = levels[0][0]


def ocean(
    theta_ref,
    mate_ref,
    next_ref,
    mate_bulk_ref,
    next_bulk_ref,
    level_ref,
    inflow_ref,
    wet_ref,
    out_ref,
    even,
    odd,
    keep,
    side,
    rise,
    source,
    sems,
):
    tiers, lines, span = theta_ref.shape
    chunks = span // LANES
    places = tiers + STEPS
    skip = STEPS + 1
    lev = lax.axis_index("lev")
    lower = lev.astype(f32)
    upper = 1.0 - lower

    wet_own = wet_ref[...].astype(f32)
    even_block = is_even()
    wet_halo = halo_rows(even_block, mate_ref[1], next_ref[1])
    flow_halo = halo_rows(even_block, mate_ref[0], next_ref[0])
    for at, wet, flow in ((0, wet_own, inflow_ref[...]), (8, wet_halo, flow_halo)):
        rows = slice(at, at + 8)
        keep[rows, :] = 1.0 - (4 * horizontal_rate + 2 * vertical_rate) * wet
        side[rows, :] = horizontal_rate * wet
        rise[rows, :] = vertical_rate * wet
        source[rows, :] = (flux_gain * upper) * (wet * flow)

    for at in range(places):
        if at >= tiers:
            even[at, 0:8, :] = level_ref[at - tiers]
        elif at in (0, tiers - 1):
            even[at, 0:8, :] = theta_ref[at]
        if at < skip:
            mate, other = mate_ref[at + 2], next_ref[at + 2]
        else:
            mate, other = mate_bulk_ref[at - skip], next_bulk_ref[at - skip]
        even[at, 8:12, :] = jnp.where(even_block, mate, other)
        even[at, 12:16, :] = jnp.where(even_block, other, mate)

    row = lax.broadcasted_iota(i32, (SUBLANES, LANES), 0)
    lane = lax.broadcasted_iota(i32, (SUBLANES, LANES), 1)
    first, last = row == 0, row == SUBLANES - 1
    lane_first, lane_last = lane == 0, lane == LANES - 1

    copies = []
    for step in range(1, STEPS + 1):
        held, fresh = (even, odd) if step % 2 else (odd, even)
        final = step == STEPS
        parts = (0,) if final else (0, 8)

        def advance(at, less, more, less_scale=None, more_scale=None, add_source=False):
            def plane(index, p, cols):
                if step == 1 and p == 0 and isinstance(index, int) and index < tiers:
                    return theta_ref[index, :, cols]
                return held[index, p : p + 8, cols]

            value = {
                (p, c): plane(at, p, slice(c * LANES, (c + 1) * LANES))
                for p in (0, 8)
                for c in range(chunks)
            }
            right = {(p, c): pltpu.roll(value[p, c], 1, 1) for p in parts for c in range(chunks)}
            left = {(p, c): pltpu.roll(value[p, c], LANES - 1, 1) for p in parts for c in range(chunks)}
            for c in range(chunks):
                cols = slice(c * LANES, (c + 1) * LANES)
                for p in parts:
                    mine, next_to = value[p, c], value[8 - p, c]
                    around = pltpu.roll(jnp.where(last, next_to, mine), 1, 0)
                    around = around + pltpu.roll(jnp.where(first, next_to, mine), 7, 0)
                    along = jnp.where(lane_first, right[p, (c - 1) % chunks], right[p, c])
                    along = along + jnp.where(lane_last, left[p, (c + 1) % chunks], left[p, c])
                    rows = slice(p, p + 8)
                    a, b = plane(less, p, cols), plane(more, p, cols)
                    if less_scale is not None:
                        a = a * less_scale
                    if more_scale is not None:
                        b = b * more_scale
                    new = (
                        keep[rows, cols] * value[p, c]
                        + side[rows, cols] * (around + along)
                        + rise[rows, cols] * (a + b)
                    )
                    if add_source:
                        new = new + source[rows, cols]
                    fresh[at, rows, cols] = new

        advance(0, places - 1, 1, less_scale=lower, add_source=True)
        for at in range(1, tiers):
            advance(at, at - 1, at + 1, more_scale=upper if at == tiers - 1 else None)
            if final and (at + 1) % STREAM == 0:
                k = at // STREAM
                some = slice(k * STREAM, (k + 1) * STREAM)
                copies.append(
                    pltpu.make_async_copy(fresh.at[some, 0:8, :], out_ref.at[some], sems.at[k])
                )
                copies[-1].start()
        for j in range(STEPS - step):
            at = tiers + j + lev * step
            more = jnp.where(at == places - 1, 0, at + 1)
            advance(at, at - 1, more)
    for copy in copies:
        copy.wait()


def entry_blocks(ref):
    rows, slots = ref.shape
    return [
        (slice(r, r + SUBLANES), slice(c, c + LANES))
        for r in range(0, rows, SUBLANES)
        for c in range(0, slots, LANES)
    ]


def picked(tables, keys, lanes):
    found = [jnp.zeros((SUBLANES, LANES), f32) for _ in keys]
    for r, table in enumerate(tables):
        spread = jnp.broadcast_to(table, (SUBLANES, LANES))
        found = [
            jnp.where(
                k == r, jnp.take_along_axis(spread, l, axis=1, mode="promise_in_bounds"), v
            )
            for k, l, v in zip(keys, lanes, found)
        ]
    return found


def own_forcing(place_ref, drive_ref, out_ref):
    rows, half = drive_ref.shape
    count = out_ref.shape[1]
    drive = jnp.concatenate(split(drive_ref[...]), axis=0)
    place = place_ref[:, 0:half]
    width = 256
    for start in range(0, count, width):
        target = start + lax.broadcasted_iota(i32, (width, half), 0)
        both = dot_nt(drive, jnp.where(target == place, 1.0, 0.0).astype(bf16))
        out_ref[:, start : start + width] = both[0:rows] + both[rows : 2 * rows]


def columns(
    state_ref,
    classes_ref,
    forcing_ref,
    far_ref,
    link_ref,
    warmth_ref,
    sender_ref,
    share_ref,
    out_ref,
    pieces_ref,
    result,
    sems,
):
    rows, count = state_ref.shape
    half = far_ref.shape[1]
    levels = rows // 2
    width = 256

    far_drive = jnp.concatenate(split(far_ref[0:rows, :]), axis=0)
    far_place = far_ref[rows : rows + 1, :].astype(i32)
    link_high, link_low = split(link_ref[...])
    link_both = jnp.concatenate([link_high, link_low], axis=0)

    chunks = [slice(start, start + width) for start in range(0, count, width)]
    forcing = []
    for cols in chunks:
        target = cols.start + lax.broadcasted_iota(i32, (width, half), 0)
        far_pick = jnp.where(target == far_place, 1.0, 0.0).astype(bf16)
        both = dot_nt(far_drive, far_pick)
        forcing.append(forcing_ref[:, cols] + (both[0:rows] + both[rows : 2 * rows]))
    states = [state_ref[:, cols] for cols in chunks]
    for k in range(CLASSES):
        for c, cols in enumerate(chunks):
            x = states[c]
            high, low = split(x)
            product = dot_nn(link_both, high)
            drive = product[0:rows] + (product[rows : 2 * rows] + dot_nn(link_high, low)) + forcing[c]
            states[c] = x + jnp.where(classes_ref[:, cols] > k, tendency_scale * jnp.tanh(drive), 0.0)
    copies = []
    flux = []
    for c, cols in enumerate(chunks):
        x = states[c]
        result[:, cols] = x
        copies.append(pltpu.make_async_copy(result.at[:, cols], out_ref.at[:, cols], sems.at[c]))
        copies[c].start()
        flux.append(
            surface_exchange_factor * (x[levels - 1 : levels, :] - warmth_ref[:, cols])
            + humidity_exchange_factor * x[rows - 1 : rows, :]
        )
    flux = jnp.concatenate(flux, axis=1)

    blocks = entry_blocks(sender_ref)
    lanes = [sender_ref[b] & (LANES - 1) for b in blocks]
    keys = [sender_ref[b] >> 7 for b in blocks]
    tables = [flux[:, r * LANES : (r + 1) * LANES] for r in range(count // LANES)]
    for b, v in zip(blocks, picked(tables, keys, lanes)):
        pieces_ref[b] = share_ref[b] * v
    for copy in copies:
        copy.wait()


def targets(tile_ref, top_ref, top_far_ref, pieces_ref, payload_ref):
    lines, span = top_ref.shape
    surface = jnp.where(lax.axis_index("lev") == 0, top_ref[...], top_far_ref[...])
    blocks = entry_blocks(tile_ref)
    lanes = [tile_ref[b] & (LANES - 1) for b in blocks]
    keys = [tile_ref[b] >> 7 for b in blocks]
    tables = [
        surface[r : r + 1, c : c + LANES] for r in range(lines) for c in range(0, span, LANES)
    ]
    for (r, c), v in zip(blocks, picked(tables, keys, lanes)):
        part = c.start // LANES
        payload_ref[pl.ds(4 * r.start + part, SUBLANES, stride=4), :] = pieces_ref[r, c]
        payload_ref[pl.ds(4 * r.start + 2 + part, SUBLANES, stride=4), :] = v


def entry_sum(index_row, value_row, groups, order, width=LANES):
    entries = index_row.shape[1]
    group = order(index_row)
    hit = lax.broadcasted_iota(i32, (groups, entries), 0) == group
    high = value_row.astype(bf16).astype(f32)
    low = value_row - high
    weighted = jnp.concatenate(
        [jnp.where(hit, high, 0.0).astype(bf16), jnp.where(hit, low, 0.0).astype(bf16)], axis=0
    )
    lane = index_row & (width - 1)
    lane_hit = lax.broadcasted_iota(i32, (width, entries), 0) == lane
    return dot_nt(weighted, jnp.where(lane_hit, 1.0, 0.0).astype(bf16))


def joined_rows(ref, at):
    return jnp.concatenate([ref[at : at + 1, :], ref[at + 1 : at + 2, :]], axis=1)


def add_flux(received_ref, tile_ref, out_ref):
    entry_rows, slots = tile_ref.shape
    lines, span = out_ref.shape
    chunks = span // LANES
    groups = lines * chunks
    total = jnp.zeros((2 * groups, LANES), f32)
    for d in range(entry_rows):
        total = total + entry_sum(
            tile_ref[d : d + 1, :],
            joined_rows(received_ref, 4 * d),
            groups,
            lambda t: ((t >> 7) & (chunks - 1)) * lines + (t >> 10),
        )
    total = total[0:groups] + total[groups:]
    for c in range(chunks):
        out_ref[:, c * LANES : (c + 1) * LANES] = total[c * lines : (c + 1) * lines]


def add_warmth(received_ref, sender_ref, share_ref, flux_ref, other_flux_ref, out_ref, rate_ref):
    rate_ref[...] = flux_ref[...] + other_flux_ref[...]
    entry_rows, slots = sender_ref.shape
    lines = out_ref.shape[0]
    parts = 4
    width = LANES // parts
    groups = lines * parts
    total = jnp.zeros((2 * groups, width), f32)
    for d in range(entry_rows):
        total = total + entry_sum(
            sender_ref[d : d + 1, :],
            joined_rows(received_ref, 4 * d + 2) * share_ref[d : d + 1, :],
            groups,
            lambda t: ((t >> 5) & (parts - 1)) * lines + (t >> 7),
            width,
        )
    total = total[0:groups] + total[groups:]
    for k in range(parts):
        out_ref[:, k * width : (k + 1) * width] = total[k * lines : (k + 1) * lines]


def on_device(
    air_profile_vector,
    profile_pass_kind,
    position_profile_map,
    sunlight_aerosol_drive,
    profile_link_operator,
    bottom_warmth_seen,
    intersect_sender_index,
    intersect_share,
    intersect_receiver_tile,
    marine_warmth_departure,
    earlier_bottom_inflow,
    marine_tile_indicator,
):
    rows, count = air_profile_vector.shape
    half = count // 2
    tiers, lines, span = marine_warmth_departure.shape
    entry_rows, slots = intersect_sender_index.shape
    n_dom = lax.axis_size("dom")
    n_block = lax.axis_size("comp") * n_dom
    place = position_profile_map.reshape(1, count)

    def shape(*dims):
        return jax.ShapeDtypeStruct(dims, f32)

    packed, mate, follow, level = call(
        pack_first,
        [
            shape(rows + SUBLANES, half),
            shape(STEPS + 3, 4, span),
            shape(STEPS + 3, 4, span),
            shape(STEPS, lines, span),
        ],
        [pl.BlockSpec(memory_space=pl.ANY)] * 5,
        (
            sunlight_aerosol_drive,
            place,
            marine_warmth_departure,
            earlier_bottom_inflow,
            marine_tile_indicator,
        ),
        "pack_first",
        1.5,
        scratch=[
            pltpu.VMEM((1, count), i32),
            pltpu.VMEM((STEPS + 1, lines, span), f32),
            pltpu.VMEM((lines, span), f32),
            pltpu.VMEM((lines, span), i32),
            pltpu.SemaphoreType.DMA((6,)),
        ],
        mib=56,
    )
    block_axes = ("comp", "dom")
    mates = [(i, i ^ 1) for i in range(n_block)]
    nexts = [(i, i + 1) for i in range(1, n_block - 1, 2)]
    nexts = nexts + [(j, i) for i, j in nexts]
    other = [(0, 1), (1, 0)]

    far = lax.ppermute(packed, "dom", [(i, (i + n_dom // 2) % n_dom) for i in range(n_dom)])
    level = lax.ppermute(level, "lev", other)
    mate = lax.ppermute(mate, block_axes, mates)
    follow = lax.ppermute(follow, block_axes, nexts)
    forcing = call(
        own_forcing,
        shape(rows, count),
        [whole(), pl.BlockSpec((rows, half), lambda i: (0, 0))],
        (place, sunlight_aerosol_drive),
        "own_forcing",
        1.0,
        grid=(1,),
    )
    air_profile_updated, pieces = call(
        columns,
        [shape(rows, count), shape(entry_rows, slots)],
        [whole()] * 8,
        (
            air_profile_vector,
            profile_pass_kind.reshape(1, count),
            forcing,
            far,
            profile_link_operator,
            bottom_warmth_seen.reshape(1, count),
            intersect_sender_index,
            intersect_share,
        ),
        "columns",
        3.0,
        scratch=[pltpu.VMEM((rows, count), f32), pltpu.SemaphoreType.DMA((count // 256,))],
        out_specs=[pl.BlockSpec(memory_space=pl.ANY), whole()],
    )
    mate, follow, pieces = lax.optimization_barrier((mate, follow, pieces))
    part = pl.BlockSpec((STEPS + 3, 4, span), lambda i: (0, 0, 0))
    top = call(
        top_level,
        shape(lines, span),
        [pl.BlockSpec((STEPS + 1, lines, span), lambda i: (0, 0, 0)), part, part, whole(), whole()],
        (marine_warmth_departure, mate, follow, earlier_bottom_inflow, marine_tile_indicator),
        "top_level",
        1.0,
        grid=(1,),
    )
    top_far = lax.ppermute(top, "lev", [(0, 1)])

    mate_bulk = call(
        functools.partial(pack_bulk, 0),
        shape(tiers - 1, 4, span),
        [whole()] * 2,
        (marine_warmth_departure, level),
        "pack_bulk_0",
        0.5,
    )
    mate_bulk = lax.ppermute(mate_bulk, block_axes, mates)
    later_level, top = lax.optimization_barrier((level, top))
    follow_bulk = call(
        functools.partial(pack_bulk, 1),
        shape(tiers - 1, 4, span),
        [whole()] * 2,
        (marine_warmth_departure, later_level),
        "pack_bulk_1",
        0.5,
    )
    follow_bulk = lax.ppermute(follow_bulk, block_axes, nexts)
    payload = call(
        targets,
        shape(4 * entry_rows, LANES),
        [whole()] * 4,
        (intersect_receiver_tile, top, top_far, pieces),
        "targets",
        8.0,
    )
    received = lax.all_to_all(
        payload.reshape(entry_rows, 4, LANES), "dom", split_axis=0, concat_axis=0, tiled=True
    ).reshape(4 * entry_rows, LANES)

    partial_flux = call(
        add_flux,
        shape(lines, span),
        [whole()] * 2,
        (received, intersect_receiver_tile),
        "add_flux",
        2.0,
    )
    late_level, partial_flux = lax.optimization_barrier((level, partial_flux))
    theta = call(
        ocean,
        shape(tiers, lines, span),
        [whole()] * 8,
        (
            marine_warmth_departure,
            mate,
            follow,
            mate_bulk,
            follow_bulk,
            late_level,
            earlier_bottom_inflow,
            marine_tile_indicator,
        ),
        "ocean",
        6.0,
        scratch=[pltpu.VMEM((tiers + STEPS, 16, span), f32)] * 2 + [pltpu.VMEM((16, span), f32)] * 4
        + [pltpu.SemaphoreType.DMA((tiers // STREAM,))],
        out_specs=[pl.BlockSpec(memory_space=pl.ANY)],
    )

    other_flux = lax.ppermute(partial_flux, "lev", other)
    theta, other_flux = lax.optimization_barrier((theta, other_flux))
    air_bottom_warmth, marine_warming_rate = call(
        add_warmth,
        [shape(count // LANES, LANES), shape(lines, span)],
        [whole()] * 5,
        (received, intersect_sender_index, intersect_share, partial_flux, other_flux),
        "add_warmth",
        2.0,
    )
    air_bottom_warmth = air_bottom_warmth.reshape(count)
    return (air_profile_updated, theta, marine_warming_rate, air_bottom_warmth)


def solution(mesh):
    placed = (
        P(None, ("comp", "dom", "lev")),
        P(("comp", "dom", "lev")),
        P(("comp", "dom", "lev")),
        P(None, ("comp", "dom", "lev")),
        P(),
        P(("comp", "dom", "lev")),
        P(("comp", "dom", "lev"), None),
        P(("comp", "dom", "lev"), None),
        P(("comp", "dom", "lev"), None),
        P("lev", ("comp", "dom"), None),
        P(("comp", "dom"), None),
        P(("comp", "dom"), None),
    )
    return jax.shard_map(
        on_device,
        mesh=mesh,
        in_specs=placed,
        out_specs=(
            P(None, ("comp", "dom", "lev")),
            P("lev", ("comp", "dom"), None),
            P(("comp", "dom"), None),
            P(("comp", "dom", "lev")),
        ),
        check_vma=False,
    )
```
